512 devices in a mesh: ctx: 32 (over y, x, core), head: 16 (over z).
Axes of the slice: x: 4, y: 4, z: 16, core: 2. Of those that a mesh axis runs over, the one named last changes fastest.
Arguments:
- queries: bfloat16 [65536, 4096], P(('ctx', 'head')), may hold values from -128 to 128
- vis_feats: bfloat16 [16384, 8192], P('ctx', 'head'), may hold values from -16 to 16
- kv_weight: bfloat16 [8192, 1024], P('head'), may hold values from -0.044194174 to 0.044194174
- key_gain: float32 [128], replicated, may hold values from 0.1 to 1.9
- cross_mask: int32 [65536, 4], P('ctx'), may hold values 0 or 1
- image_tokens: int32 [4], replicated, may hold values from 1 to 512, 1280 in all
- image_owner: int32 [4], replicated, may hold values from 0 to 31, as said below
Outputs:
- attended: bfloat16 [65536, 4096], P(('ctx', 'head'))
The draws below stay inside these ranges and needn't reach their ends.
Inputs may be any that keep to these rules, and one draw needn't show every extreme that they name: `image_tokens`: they sum to 1280; the largest is exactly 512. `image_owner`: four distinct context indices; the first and the last index of ctx always hold an image.
All inputs are finite; a program needn't handle non-finite values. No bound on the sum of `cross_mask` on one device may be relied on, other than what follows from the above.
Results may differ from the reference program's by a relative error of at most 0.0014.
The reference program's roundings to bfloat16 on the way count: a program that leaves them out, or rounds other values in their place, can miss the bound.
Values may be sent and summed in bfloat16 or wider, within the bound.
A program may use at most 64 MiB of HBM per device.

```python
import math
import jax
import jax.numpy as jnp
import numpy as np
from jax import lax

MODEL_WIDTH = 8192
HEAD_SIZE = 128
QUERY_HEAD_COUNT = 32
KEY_VALUE_HEADS = 4
NIMG = 4
IMAGE_TOKEN_MAX = 512
KV_TOTAL = 1280
TOKENS = 65536
N_CTX = 32


def shared_parts(key):
    weight_matrix = jnp.clip(jax.random.normal(jax.random.fold_in(key, 12), (MODEL_WIDTH, 2 * KEY_VALUE_HEADS * HEAD_SIZE), jnp.float32), -4.0, 4.0) * MODEL_WIDTH ** (-0.5)
    return weight_matrix


def draw_kv_weight(key, part):
    return shared_parts(key).astype(jnp.bfloat16)


def draw_vis_feats(key, part):
    noise = jnp.clip(jax.random.normal(jax.random.fold_in(key, 13), (N_CTX * IMAGE_TOKEN_MAX, MODEL_WIDTH), jnp.float32), -4.0, 4.0)
    return noise.astype(jnp.bfloat16)


def draw_queries(key, part):
    drawn = jnp.clip(jax.random.normal(jax.random.fold_in(key, 14), (TOKENS, QUERY_HEAD_COUNT * HEAD_SIZE), jnp.float32), -4.0, 4.0)
    return drawn.astype(jnp.bfloat16)


def draw_image_owner(key, part):
    middle = jax.random.permutation(jax.random.fold_in(key, 21), N_CTX - 2)[:2] + 1
    chosen = jnp.concatenate([jnp.array([0, N_CTX - 1], dtype=jnp.int32), middle.astype(jnp.int32)])
    return jax.random.permutation(jax.random.fold_in(key, 22), chosen).astype(jnp.int32)


def set_ends(values, own_key, least, high):
    longest = values.shape.index(max(values.shape))
    spots = []
    for shift in (0, 1):
        where = [jax.random.randint(jax.random.fold_in(own_key, axis), (), 0, length) for axis, length in enumerate(values.shape)]
        where[longest] = (where[longest] + shift) % values.shape[longest]
        spots.append(tuple(where))
    return values.at[spots[0]].set(least).at[spots[1]].set(high)


def split_up(count, total, most, skew):
    loads = [(1 << 20) // math.isqrt(rank ** skew) + 1 for rank in range(2, count + 1)]
    rest, given = total - most - (count - 1), [1] * (count - 1)
    while rest > 0:
        free = [i for i in range(count - 1) if given[i] < most]
        whole, budget = sum([loads[i] for i in free]), rest
        for i in free:
            addition = min(most - given[i], max(1, budget * loads[i] // whole), rest)
            given[i] = given[i] + addition
            rest = rest - addition
    return np.array([most] + given)


def uneven_parts(stream_key, count, total, bound, skew):
    if count == 2:
        one = jax.random.randint(stream_key, (), max(1, total - bound), min(bound, total - 1) + 1)
        return jnp.stack([one, total - one])
    sizes = jnp.asarray(split_up(count, total, bound, skew), jnp.int32)
    pairs = (count - 1) // 2
    source_of, sink = sizes[1:1 + 2 * pairs:2], sizes[2:2 + 2 * pairs:2]
    slack = jnp.minimum(source_of - 1, bound - sink)
    moved = jax.random.randint(jax.random.fold_in(stream_key, 1), (pairs,), 0, 1 << 20) % (slack + 1)
    sizes = sizes.at[1:1 + 2 * pairs:2].set(source_of - moved).at[2:2 + 2 * pairs:2].set(sink + moved)
    return sizes[jax.random.permutation(jax.random.fold_in(stream_key, 2), count)]


def setup_inputs(seed: int = 0) -> dict:
    arg_keys = jax.random.split(jax.random.key(seed), 8)
    queries = draw_queries(jax.random.fold_in(arg_keys[7], 71), 0)
    vis_feats = draw_vis_feats(jax.random.fold_in(arg_keys[7], 71), 0)
    kv_weight = draw_kv_weight(jax.random.fold_in(arg_keys[7], 71), 0)
    key_gain = jnp.clip(1.0 + 0.18 * jax.random.normal(arg_keys[3], (HEAD_SIZE,), jnp.float32), 0.1, 1.9)
    cross_mask = set_ends((jax.random.randint(arg_keys[4], (TOKENS, NIMG), 0, 4) < 3).astype(jnp.int32), jax.random.fold_in(arg_keys[4], 1), 0, 1)
    image_tokens = uneven_parts(arg_keys[5], NIMG, KV_TOTAL, IMAGE_TOKEN_MAX, 2).astype(jnp.int32)
    image_owner = draw_image_owner(jax.random.fold_in(arg_keys[7], 71), 0)
    return {"queries": queries, "vis_feats": vis_feats, "kv_weight": kv_weight, "key_gain": key_gain, "cross_mask": cross_mask, "image_tokens": image_tokens, "image_owner": image_owner}


EPSILON = 1e-05

def project_image(vis_feats, kv_weight, key_gain, owner_idx):
    first_row = (owner_idx * IMAGE_TOKEN_MAX).astype(jnp.int32)
    rows_img = lax.dynamic_slice_in_dim(vis_feats, first_row, IMAGE_TOKEN_MAX, 0)
    projected_rows = jnp.dot(rows_img, kv_weight, preferred_element_type=jnp.float32)
    projected_rows = projected_rows.reshape(IMAGE_TOKEN_MAX, KEY_VALUE_HEADS, 2, HEAD_SIZE)
    raw_keys = projected_rows[:, :, 0, :]
    square_mean = lax.optimization_barrier(jnp.mean(raw_keys * raw_keys, axis=-1, keepdims=True))
    normed = raw_keys * lax.rsqrt(square_mean + EPSILON) * key_gain
    return (normed.astype(jnp.bfloat16), projected_rows[:, :, 1, :].astype(jnp.bfloat16))

def reference(queries, vis_feats, kv_weight, key_gain, cross_mask, image_tokens, image_owner):
    key_parts = []
    value_parts = []
    for img_index in range(NIMG):
        normed, values = project_image(vis_feats, kv_weight, key_gain, image_owner[img_index])
        key_parts.append(normed)
        value_parts.append(values)
    key_all = lax.optimization_barrier(jnp.concatenate(key_parts, 0)).astype(jnp.float32)
    value_all = lax.optimization_barrier(jnp.concatenate(value_parts, 0)).astype(jnp.float32)
    positions = jnp.arange(NIMG * IMAGE_TOKEN_MAX, dtype=jnp.int32)
    key_image = positions // IMAGE_TOKEN_MAX
    key_slot = positions % IMAGE_TOKEN_MAX
    key_valid = key_slot < image_tokens[key_image]
    onehot = ((key_image[:, None] == jnp.arange(NIMG, dtype=jnp.int32)[None, :]) & key_valid[:, None]).astype(jnp.float32)
    rows_per_block = min(1024, TOKENS)
    count_of_blocks = TOKENS // rows_per_block
    blocked_queries = queries.reshape(count_of_blocks, rows_per_block, KEY_VALUE_HEADS, QUERY_HEAD_COUNT // KEY_VALUE_HEADS, HEAD_SIZE)
    mask_blocks = cross_mask.reshape(count_of_blocks, rows_per_block, NIMG)
    factor = HEAD_SIZE ** (-0.5)

    def one_block(block_pair):
        query_block, mask_block = block_pair
        allowed = jnp.dot(mask_block.astype(jnp.float32), onehot.T) > 0.5
        allowed = allowed[:, None, None, :]
        scores = jnp.einsum('rkgd,tkd->rkgt', query_block.astype(jnp.float32), key_all) * factor
        largest = lax.optimization_barrier(jnp.max(jnp.where(allowed, scores, -1e+30), axis=-1, keepdims=True))
        weights = jnp.where(allowed, jnp.exp(scores - largest), 0.0)
        summed = lax.optimization_barrier(jnp.sum(weights, axis=-1, keepdims=True))
        rounded = lax.optimization_barrier(weights.astype(jnp.bfloat16)).astype(jnp.float32)
        mixed_out = jnp.einsum('rkgt,tkd->rkgd', rounded, value_all) / jnp.maximum(summed, 1.0)
        return mixed_out.astype(jnp.bfloat16).reshape(rows_per_block, QUERY_HEAD_COUNT * HEAD_SIZE)
    return lax.map(one_block, (blocked_queries, mask_blocks)).reshape(TOKENS, QUERY_HEAD_COUNT * HEAD_SIZE)
```

```python
import functools
import math

import jax
import jax.numpy as jnp
from jax import lax
from jax.experimental import pallas as pl
from jax.experimental.pallas import tpu as pltpu
from jax.sharding import PartitionSpec as P

EPSILON = 1e-05
FLOOR_SCORE = -1e30
MASKED = -(2.0**120)
HEAD = 128
PACKED = 1280


def packed_index(image_tokens):
    images = jnp.arange(image_tokens.shape[0], dtype=jnp.int32)
    earlier = images[None, :] < images[:, None]
    starts = jnp.sum(jnp.where(earlier, image_tokens[None, :], 0), axis=1)
    ends = starts + image_tokens
    place = jnp.arange(PACKED, dtype=jnp.int32)
    image = jnp.sum((place[:, None] >= ends[None, :]).astype(jnp.int32), axis=1)
    onehot = image[:, None] == images[None, :]
    token = place - jnp.sum(jnp.where(onehot, starts[None, :], 0), axis=1)
    return onehot, token


def attend_kernel(group, q_ref, kv_ref, mask_ref, hot_ref, o_ref, keys):
    rows = q_ref.shape[0]
    heads = kv_ref.shape[1] // (2 * HEAD)
    per_step = 4
    factor = HEAD**-0.5 * math.log2(math.e)
    bias = mask_ref[...]
    keys[:, HEAD:] = hot_ref[...]
    for head in range(heads):
        keys[:, :HEAD] = kv_ref[:, 2 * head * HEAD : (2 * head + 1) * HEAD]
        values = kv_ref[:, (2 * head + 1) * HEAD : (2 * head + 2) * HEAD]

        def step(i, carry):
            base = pl.multiple_of((head * group + i * per_step) * HEAD, HEAD)
            stacked = jnp.concatenate(
                [
                    jnp.concatenate([q_ref[:, pl.ds(base + j * HEAD, HEAD)], bias], axis=1)
                    for j in range(per_step)
                ],
                axis=0,
            )
            scores = lax.dot_general(
                stacked, keys[...], (((1,), (1,)), ((), ())), preferred_element_type=jnp.float32
            )
            largest = jnp.maximum(jnp.max(scores, axis=1, keepdims=True), FLOOR_SCORE)
            weights = jnp.exp2(scores * factor - largest * factor)
            summed = jnp.sum(weights, axis=1, keepdims=True)
            mixed = jnp.dot(weights.astype(jnp.bfloat16), values, preferred_element_type=jnp.float32)
            out = (mixed / jnp.maximum(summed, 1.0)).astype(jnp.bfloat16)
            for j in range(per_step):
                o_ref[:, pl.ds(base + j * HEAD, HEAD)] = out[j * rows : (j + 1) * rows]
            return carry

        lax.fori_loop(0, group // per_step, step, 0)


def attend(queries, kv, bias, hot, group):
    return pl.pallas_call(
        functools.partial(attend_kernel, group),
        out_shape=jax.ShapeDtypeStruct(queries.shape, jnp.bfloat16),
        in_specs=[pl.BlockSpec(memory_space=pltpu.VMEM)] * 4,
        out_specs=pl.BlockSpec(memory_space=pltpu.VMEM),
        scratch_shapes=[pltpu.VMEM((PACKED, 2 * HEAD), jnp.bfloat16)],
        compiler_params=pltpu.CompilerParams(vmem_limit_bytes=56 * 1024 * 1024),
        name="attend",
    )(queries, kv, bias, hot)


def shards(queries, vis_feats, kv_weight, key_gain, cross_mask, image_tokens, image_owner):
    ctx, z = lax.axis_index("ctx"), lax.axis_index("head")
    rows = queries.shape[0]
    onehot, token = packed_index(image_tokens)
    owned = jnp.sum(jnp.where(onehot, image_owner[None, :], 0), axis=1) == ctx
    slots = jnp.arange(vis_feats.shape[0], dtype=jnp.int32)
    select = (token[:, None] == slots[None, :]) & owned[:, None]
    contribution = jnp.dot(
        select.astype(jnp.bfloat16), vis_feats, preferred_element_type=jnp.float32
    ).astype(jnp.bfloat16)
    mine = lax.psum_scatter(contribution, "ctx", scatter_dimension=0, tiled=True)
    partial = jnp.dot(mine, kv_weight, preferred_element_type=jnp.float32)
    projected = lax.psum(partial, "head").reshape(mine.shape[0], -1, 2, HEAD)
    raw = projected[:, :, 0]
    scale = lax.rsqrt(jnp.mean(raw * raw, axis=-1, keepdims=True) + EPSILON)
    normed = raw * scale * key_gain
    kv = jnp.stack([normed, projected[:, :, 1]], axis=2).astype(jnp.bfloat16)
    kv = lax.all_gather(kv.reshape(mine.shape[0], -1), "ctx", axis=0, tiled=True)
    mask_rows = lax.dynamic_slice_in_dim(cross_mask, z * rows, rows, 0)
    bias = jnp.where(mask_rows == 1, 0.0, MASKED).astype(jnp.bfloat16)
    pad = ((0, 0), (0, HEAD - bias.shape[1]))
    bias = jnp.pad(bias, pad)
    hot = jnp.pad(onehot.astype(jnp.bfloat16), pad)
    group = queries.shape[1] // HEAD // (kv_weight.shape[1] // (2 * HEAD))
    return attend(queries, kv, bias, hot, group)


def solution(mesh):
    return jax.shard_map(
        shards,
        mesh=mesh,
        in_specs=(
            P(("ctx", "head"), None),
            P("ctx", "head"),
            P("head", None),
            P(),
            P("ctx", None),
            P(),
            P(),
        ),
        out_specs=P(("ctx", "head"), None),
        check_vma=False,
    )
```

```python
import math

import jax
import jax.numpy as jnp
from jax import lax
from jax.experimental import pallas as pl
from jax.experimental.pallas import tpu as pltpu
from jax.sharding import PartitionSpec as P

EPSILON = 1e-05
FLOOR_SCORE = -1e30
MASKED = -(2.0**120)
HEAD = 128
SIDE = 4
DEPTH = 16
SHARE = 80
PACKED = SHARE * SIDE * SIDE
GROUP = 8
STEP_HEADS = 4
MESH = pl.DeviceIdType.MESH
BF16, F32 = jnp.bfloat16, jnp.float32


def kernel(
    tokens_ref, owner_ref, feats_ref, weight_ref, gain_ref, mask_ref, q_ref, o_ref,
    own, sib, first_in, first_sum, second_in, chip_feats, part, part_in, done, kv, hot, keys,
    sib_s, sib_r, first_s, first_r, second_s, second_r, pair_s, pair_r,
    part_s, part_r, column_s, column_r, row_s, row_r, plane_s, plane_r, twin_s, twin_r,
):
    ctx, z = lax.axis_index("ctx"), lax.axis_index("head")
    core = lax.rem(ctx, 2)
    x = lax.rem(lax.div(ctx, 2), SIDE)
    y = lax.div(ctx, 2 * SIDE)
    a = x * (1 - core) + y * core
    b = y * (1 - core) + x * core

    def at(x_to, y_to, core_to, z_to):
        return {"ctx": (y_to * SIDE + x_to) * 2 + core_to, "head": z_to}

    def along_a(d):
        to = lax.rem(a + d, SIDE)
        return at(to * (1 - core) + x * core, y * (1 - core) + to * core, core, z)

    def along_b(d):
        to = lax.rem(b + d, SIDE)
        return at(x * (1 - core) + to * core, to * (1 - core) + y * core, core, z)

    def along_z(d):
        return at(x, y, core, lax.rem(z + d, DEPTH))

    twin = at(x, y, 1 - core, z)

    def chip_of(which, a_to, b_to):
        return (a_to * SIDE + b_to) * (1 - which) + (b_to * SIDE + a_to) * which

    def copy(src, dst, send, recv, device):
        return pltpu.make_async_remote_copy(
            src_ref=src, dst_ref=dst, send_sem=send, recv_sem=recv,
            device_id=device, device_id_type=MESH,
        )

    barrier = pltpu.get_barrier_semaphore()
    greeted = (
        [twin]
        + [along_a(d) for d in range(1, SIDE)]
        + [along_b(d) for d in range(1, SIDE)]
        + [along_z(d) for d in range(1, DEPTH)]
    )
    for device in greeted:
        pl.semaphore_signal(barrier, inc=1, device_id=device, device_id_type=MESH)

    images = tokens_ref.shape[0]
    starts, ends, total = [], [], jnp.int32(0)
    my_start, my_count = jnp.int32(0), jnp.int32(0)
    for i in range(images):
        starts.append(total)
        mine = owner_ref[i] == ctx
        my_start = jnp.where(mine, total, my_start)
        my_count = jnp.where(mine, tokens_ref[i], my_count)
        total = total + tokens_ref[i]
        ends.append(total)

    slots = feats_ref.shape[0]
    half = feats_ref.shape[1] // 2
    row_id = lax.broadcasted_iota(jnp.int32, (SHARE, slots), 0)
    slot_id = lax.broadcasted_iota(jnp.int32, (SHARE, slots), 1)
    distance = jnp.where(slot_id < my_count, row_id - slot_id, jnp.int32(1 << 20))

    def packed_rows(which, a_to, part_of):
        select = jnp.concatenate(
            [
                jnp.where(
                    distance == my_start - chip_of(which, a_to, b_to) * SHARE, 1.0, 0.0
                ).astype(BF16)
                for b_to in range(SIDE)
            ],
            axis=0,
        )
        columns = feats_ref[:, pl.ds(pl.multiple_of(part_of * half, half), half)]
        return jnp.dot(select, columns, preferred_element_type=F32).astype(BF16)

    for a_to in range(SIDE):
        own[a_to] = packed_rows(1 - core, a_to, 1 - core)
    pl.semaphore_wait(barrier, len(greeted))
    to_twin = [
        copy(own.at[i], sib.at[i], sib_s.at[i], sib_r.at[i], twin) for i in range(SIDE)
    ]
    for c in to_twin:
        c.start()
    for a_to in range(SIDE):
        keys_rows = packed_rows(core, a_to, core)
        first_sum[a_to] = keys_rows
    for c in to_twin:
        c.wait()
    for a_to in range(SIDE):
        first_sum[a_to] = first_sum[a_to] + sib[a_to]
    sends = [
        copy(
            first_sum.at[lax.rem(a + d, SIDE)], first_in.at[d - 1],
            first_s.at[d - 1], first_r.at[d - 1], along_a(d),
        )
        for d in range(1, SIDE)
    ]
    for c in sends:
        c.start()

    lane = lax.broadcasted_iota(jnp.int32, (SHARE, HEAD), 1)
    row = lax.broadcasted_iota(jnp.int32, (SHARE, HEAD), 0)
    begin_of, end_of = jnp.zeros_like(lane), jnp.zeros_like(lane)
    for i in range(images):
        begin_of = jnp.where(lane == i, starts[i], begin_of)
        end_of = jnp.where(lane == i, ends[i], end_of)
    for which in range(2):
        for b_to in range(SIDE):
            for a_to in range(SIDE):
                place = row + chip_of(which, a_to, b_to) * SHARE
                inside = (place >= begin_of) & (place < end_of)
                base = (b_to * SIDE + a_to) * SHARE
                hot[which, base : base + SHARE, :] = jnp.where(inside, 1.0, 0.0).astype(BF16)

    for c in sends:
        c.wait()
    block = first_sum[a]
    for d in range(1, SIDE):
        block = block + first_in[d - 1]
    for i in range(SIDE):
        own[0, i * SHARE : (i + 1) * SHARE] = block[i * SHARE : (i + 1) * SHARE]

    def share_of(i):
        return own.at[0, pl.ds(pl.multiple_of(i * SHARE, 16), SHARE)]

    sends = [
        copy(
            share_of(lax.rem(b + d, SIDE)), second_in.at[d - 1],
            second_s.at[d - 1], second_r.at[d - 1], along_b(d),
        )
        for d in range(1, SIDE)
    ]
    for c in sends:
        c.start()
    for c in sends:
        c.wait()
    block = share_of(b)[...]
    for d in range(1, SIDE):
        block = block + second_in[d - 1]
    chip_feats[core] = block
    pair = copy(chip_feats.at[core], chip_feats.at[core], pair_s.at[0], pair_r.at[0], twin)
    pair.start()
    pair.wait()

    width = weight_ref.shape[1] // 2
    blocks = width // HEAD
    columns = pl.ds(pl.multiple_of(core * width, width), width)
    product = jnp.dot(
        chip_feats[0], weight_ref[:half, columns], preferred_element_type=F32
    ) + jnp.dot(chip_feats[1], weight_ref[half:, columns], preferred_element_type=F32)
    spacing = DEPTH // blocks
    offset = core * (spacing // 2)
    for j in range(blocks):
        part[j] = product[:, j * HEAD : (j + 1) * HEAD]
    for j in range(blocks):
        home = offset + j * spacing
        d = lax.rem(home - z + DEPTH, DEPTH)

        @pl.when(d != 0)
        def _():
            copy(part.at[j], part_in.at[d], part_s.at[j], part_r.at[d], at(x, y, core, home)).start()

    is_home = lax.rem(z, spacing) == offset
    my_block = lax.div(z, spacing)

    @pl.when(is_home)
    def _():
        total = part[my_block]
        for d in range(1, DEPTH):
            copy(
                part.at[0], part_in.at[d], part_s.at[0], part_r.at[d], along_z(1)
            ).wait_recv()
        for d in range(1, DEPTH):
            total = total + part_in[d]
        scale = lax.rsqrt(jnp.mean(total * total, axis=1, keepdims=True) + EPSILON)
        normed = total * scale * gain_ref[...]
        done[...] = jnp.where(lax.rem(my_block, 2) == 0, normed, total).astype(BF16)
        for d in range(1, DEPTH):
            copy(
                done, kv.at[core, my_block, b, a], column_s.at[d - 1],
                column_r.at[my_block], along_z(d),
            ).start()
        kv[core, my_block, b, a] = done[...]

    row_copies, plane_copies, twin_copies = [], [], []
    for h in range(blocks // 2):
        pieces = pl.ds(2 * h, 2)
        row_copies.append(
            [
                copy(
                    kv.at[core, pieces, b, a], kv.at[core, pieces, b, a],
                    row_s.at[h, d - 1], row_r.at[h, d - 1], along_a(d),
                )
                for d in range(1, SIDE)
            ]
        )
        plane_copies.append(
            [
                copy(
                    kv.at[core, pieces, b], kv.at[core, pieces, b],
                    plane_s.at[h, d - 1], plane_r.at[h, d - 1], along_b(d),
                )
                for d in range(1, SIDE)
            ]
        )
        twin_copies.append(
            copy(kv.at[core, pieces], kv.at[core, pieces], twin_s.at[h], twin_r.at[h], twin)
        )

    for h in range(blocks // 2):
        for j in (2 * h, 2 * h + 1):

            @pl.when(jnp.logical_not(is_home & (my_block == j)))
            def _():
                copy(
                    done, kv.at[core, j, b, a], column_s.at[0], column_r.at[j], along_z(1)
                ).wait_recv()

        for c in row_copies[h]:
            c.start()
    for h in range(blocks // 2):
        for c in row_copies[h]:
            c.wait_recv()
        for c in plane_copies[h]:
            c.start()

    lanes = lax.broadcasted_iota(jnp.int32, mask_ref.shape[:1] + (HEAD,), 1)
    bias = jnp.zeros(lanes.shape, F32)
    for i in range(images):
        bias = jnp.where((lanes == i) & (mask_ref[:, i : i + 1] != 1), MASKED, bias)
    bias = bias.astype(BF16)
    rows = q_ref.shape[0]
    factor = HEAD**-0.5 * math.log2(math.e)

    def attend(which, h):
        keys[:, :HEAD] = kv[which, 2 * h].reshape(PACKED, HEAD)
        keys[:, HEAD:] = hot[which]

        def step(i, carry):
            head = (which * (blocks // 2) + h) * GROUP + i * STEP_HEADS
            base = pl.multiple_of(head * HEAD, HEAD)
            stacked = jnp.concatenate(
                [
                    jnp.concatenate([q_ref[:, pl.ds(base + n * HEAD, HEAD)], bias], axis=1)
                    for n in range(STEP_HEADS)
                ],
                axis=0,
            )
            scores = lax.dot_general(
                stacked, keys[...], (((1,), (1,)), ((), ())), preferred_element_type=F32
            )
            largest = jnp.maximum(jnp.max(scores, axis=1, keepdims=True), FLOOR_SCORE)
            weights = jnp.exp2(scores * factor - largest * factor)
            summed = jnp.sum(weights, axis=1, keepdims=True)
            mixed = jnp.dot(
                weights.astype(BF16), kv[which, 2 * h + 1].reshape(PACKED, HEAD),
                preferred_element_type=F32,
            )
            out = (mixed / jnp.maximum(summed, 1.0)).astype(BF16)
            for n in range(STEP_HEADS):
                o_ref[:, pl.ds(base + n * HEAD, HEAD)] = out[n * rows : (n + 1) * rows]
            return carry

        lax.fori_loop(0, GROUP // STEP_HEADS, step, 0)

    for h in range(blocks // 2):
        for c in plane_copies[h]:
            c.wait_recv()
        twin_copies[h].start()
        attend(core, h)
    for h in range(blocks // 2):
        twin_copies[h].wait_recv()
        attend(1 - core, h)

    for h in range(blocks // 2):
        twin_copies[h].wait_send()
        for c in row_copies[h] + plane_copies[h]:
            c.wait_send()
    for j in range(blocks):
        home = offset + j * spacing

        @pl.when(z != home)
        def _():
            copy(
                part.at[j], part_in.at[1], part_s.at[j], part_r.at[1], along_z(1)
            ).wait_send()

    @pl.when(is_home)
    def _():
        for d in range(1, DEPTH):
            copy(
                done, kv.at[core, my_block, b, a], column_s.at[d - 1],
                column_r.at[my_block], along_z(d),
            ).wait_send()


def shards(queries, vis_feats, kv_weight, key_gain, cross_mask, image_tokens, image_owner):
    z = lax.axis_index("head")
    rows = queries.shape[0]
    mask_rows = lax.dynamic_slice_in_dim(cross_mask, z * rows, rows, 0)
    half = vis_feats.shape[1] // 2
    blocks = kv_weight.shape[1] // (2 * HEAD)
    dma = pltpu.SemaphoreType.DMA
    whole = pl.BlockSpec(memory_space=pltpu.VMEM)
    scalars = pl.BlockSpec(memory_space=pltpu.SMEM)
    return pl.pallas_call(
        kernel,
        out_shape=jax.ShapeDtypeStruct(queries.shape, BF16),
        in_specs=[scalars, scalars, whole, whole, whole, whole, whole],
        out_specs=whole,
        scratch_shapes=[
            pltpu.VMEM((SIDE, SIDE * SHARE, half), BF16),
            pltpu.VMEM((SIDE, SIDE * SHARE, half), BF16),
            pltpu.VMEM((SIDE - 1, SIDE * SHARE, half), BF16),
            pltpu.VMEM((SIDE, SIDE * SHARE, half), BF16),
            pltpu.VMEM((SIDE - 1, SHARE, half), BF16),
            pltpu.VMEM((2, SHARE, half), BF16),
            pltpu.VMEM((blocks, SHARE, HEAD), F32),
            pltpu.VMEM((DEPTH, SHARE, HEAD), F32),
            pltpu.VMEM((SHARE, HEAD), BF16),
            pltpu.VMEM((2, blocks, SIDE, SIDE, SHARE, HEAD), BF16),
            pltpu.VMEM((2, PACKED, HEAD), BF16),
            pltpu.VMEM((PACKED, 2 * HEAD), BF16),
            dma((SIDE,)), dma((SIDE,)),
            dma((SIDE - 1,)), dma((SIDE - 1,)),
            dma((SIDE - 1,)), dma((SIDE - 1,)),
            dma((1,)), dma((1,)),
            dma((blocks,)), dma((DEPTH,)),
            dma((DEPTH - 1,)), dma((blocks,)),
            dma((blocks // 2, SIDE - 1)), dma((blocks // 2, SIDE - 1)),
            dma((blocks // 2, SIDE - 1)), dma((blocks // 2, SIDE - 1)),
            dma((blocks // 2,)), dma((blocks // 2,)),
        ],
        compiler_params=pltpu.CompilerParams(
            collective_id=0, has_side_effects=True, vmem_limit_bytes=56 * 1024 * 1024
        ),
        name="cross_attend",
    )(
        image_tokens, image_owner, vis_feats, kv_weight, key_gain.reshape(1, HEAD), mask_rows,
        queries,
    )


def solution(mesh):
    return jax.shard_map(
        shards,
        mesh=mesh,
        in_specs=(
            P(("ctx", "head"), None),
            P("ctx", "head"),
            P("head", None),
            P(),
            P("ctx", None),
            P(),
            P(),
        ),
        out_specs=P(("ctx", "head"), None),
        check_vma=False,
    )
```

```python
import math

import jax
import jax.numpy as jnp
from jax import lax
from jax.experimental import pallas as pl
from jax.experimental.pallas import tpu as pltpu
from jax.sharding import PartitionSpec as P

EPSILON = 1e-05
FLOOR_SCORE = -1e30
MASKED = -(2.0**120)
HEAD = 128
SIDE = 4
DEPTH = 16
SHARE = 80
PACKED = SHARE * SIDE * SIDE
GROUP = 8
STEP_HEADS = 4
MESH = pl.DeviceIdType.MESH
BF16, F32 = jnp.bfloat16, jnp.float32


def kernel(
    tokens_ref, owner_ref, gain_ref, mask_ref, feats_hbm, weight_hbm, q_hbm, o_ref,
    feats, weight, q_ref, own, sib, first_sum, first_in, second_out, second_in, part, part_in,
    done, kv, hot, keys, rounded, divisor,
    load_s, sib_s, sib_r, first_s, first_r, second_s, second_r,
    part_s, part_r, column_s, column_r, row_s, row_r, plane_s, plane_r, twin_s, twin_r,
):
    ctx, z = lax.axis_index("ctx"), lax.axis_index("head")
    core = lax.rem(ctx, 2)
    x = lax.rem(lax.div(ctx, 2), SIDE)
    y = lax.div(ctx, 2 * SIDE)
    a = x * (1 - core) + y * core
    b = y * (1 - core) + x * core

    def at(x_to, y_to, core_to, z_to):
        return {"ctx": (y_to * SIDE + x_to) * 2 + core_to, "head": z_to}

    def along_a(d, core_to=core):
        to = lax.rem(a + d, SIDE)
        return at(to * (1 - core) + x * core, y * (1 - core) + to * core, core_to, z)

    def along_b(d, core_to=core):
        to = lax.rem(b + d, SIDE)
        return at(x * (1 - core) + to * core, to * (1 - core) + y * core, core_to, z)

    def along_z(d):
        return at(x, y, core, lax.rem(z + d, DEPTH))

    twin = at(x, y, 1 - core, z)

    def chip_of(which, a_to, b_to):
        return (a_to * SIDE + b_to) * (1 - which) + (b_to * SIDE + a_to) * which

    def copy(src, dst, send, recv, device):
        return pltpu.make_async_remote_copy(
            src_ref=src, dst_ref=dst, send_sem=send, recv_sem=recv,
            device_id=device, device_id_type=MESH,
        )

    barrier = pltpu.get_barrier_semaphore()
    greeted = (
        [twin]
        + [along_a(d) for d in range(1, SIDE)]
        + [along_b(d) for d in range(1, SIDE)]
        + [along_a(d, 1 - core) for d in range(1, SIDE)]
        + [along_z(d) for d in range(1, DEPTH)]
    )
    for device in greeted:
        pl.semaphore_signal(barrier, inc=1, device_id=device, device_id_type=MESH)
    width = weight.shape[1]
    loads = [
        pltpu.make_async_copy(feats_hbm, feats, load_s.at[0]),
        pltpu.make_async_copy(
            weight_hbm.at[:, pl.ds(pl.multiple_of(core * width, width), width)],
            weight, load_s.at[1],
        ),
        pltpu.make_async_copy(q_hbm, q_ref, load_s.at[2]),
    ]
    for c in loads:
        c.start()

    images = tokens_ref.shape[0]
    starts, ends, total = [], [], jnp.int32(0)
    my_start, my_count = jnp.int32(0), jnp.int32(0)
    for i in range(images):
        starts.append(total)
        mine = owner_ref[i] == ctx
        my_start = jnp.where(mine, total, my_start)
        my_count = jnp.where(mine, tokens_ref[i], my_count)
        total = total + tokens_ref[i]
        ends.append(total)

    slots = feats.shape[0]
    half = feats.shape[1] // 2
    row_id = lax.broadcasted_iota(jnp.int32, (SHARE, slots), 0)
    slot_id = lax.broadcasted_iota(jnp.int32, (SHARE, slots), 1)
    distance = jnp.where(slot_id < my_count, row_id - slot_id, jnp.int32(1 << 20))

    def packed_rows(which, b_to, part_of):
        select = jnp.concatenate(
            [
                jnp.where(
                    distance == my_start - chip_of(which, a_to, b_to) * SHARE, 1.0, 0.0
                ).astype(BF16)
                for a_to in range(SIDE)
            ],
            axis=0,
        )
        columns = feats[:, pl.ds(pl.multiple_of(part_of * half, half), half)]
        rows_of = jnp.dot(select, columns, preferred_element_type=F32).astype(BF16)
        return rows_of.reshape(SIDE, SHARE, half)

    order = list(range(1, SIDE)) + [0]
    to_twin = [copy(own.at[e], sib.at[e], sib_s.at[e], sib_r.at[e], twin) for e in range(SIDE)]
    loads[0].wait()
    for n, e in enumerate(order):
        own[e] = packed_rows(1 - core, lax.rem(a + e, SIDE), 1 - core)
        if n == 0:
            pl.semaphore_wait(barrier, len(greeted))
        to_twin[e].start()
    for e in order:
        first_sum[e] = packed_rows(core, lax.rem(b + e, SIDE), core)
    first = {}
    for e in order:
        to_twin[e].wait_recv()
        first_sum[e] = first_sum[e] + sib[e]
        for d in range(1, SIDE):
            first[d, e] = copy(
                first_sum.at[e, lax.rem(a + d, SIDE)], first_in.at[d - 1, e],
                first_s.at[d - 1, e], first_r.at[d - 1, e], along_a(d),
            )
            first[d, e].start()

    lane = lax.broadcasted_iota(jnp.int32, (SHARE, HEAD), 1)
    row = lax.broadcasted_iota(jnp.int32, (SHARE, HEAD), 0)
    begin_of, end_of = jnp.zeros_like(lane), jnp.zeros_like(lane)
    for i in range(images):
        begin_of = jnp.where(lane == i, starts[i], begin_of)
        end_of = jnp.where(lane == i, ends[i], end_of)
    for which in range(2):
        for b_to in range(SIDE):
            for a_to in range(SIDE):
                place = row + chip_of(which, a_to, b_to) * SHARE
                inside = (place >= begin_of) & (place < end_of)
                base = (b_to * SIDE + a_to) * SHARE
                hot[which, base : base + SHARE, :] = jnp.where(inside, 1.0, 0.0).astype(BF16)
    bias_of = jnp.where(
        mask_ref[:, pl.ds(pl.multiple_of(z * HEAD, HEAD), HEAD)] == 1, 0.0, MASKED
    ).astype(BF16)
    same = lax.broadcasted_iota(jnp.int32, (images, HEAD), 0) == lax.broadcasted_iota(
        jnp.int32, (images, HEAD), 1
    )
    bias = lax.dot_general(
        bias_of, jnp.where(same, 1.0, 0.0).astype(BF16), (((0,), (0,)), ((), ())),
        preferred_element_type=F32,
    ).astype(BF16)

    second, arrivals = [], []
    for e in order:
        for d in range(1, SIDE):
            first[d, e].wait_recv()
        block = first_sum[e, a]
        for d in range(1, SIDE):
            block = block + first_in[d - 1, e]
        if e:
            second_out[e] = block
            source, targets = second_out.at[e], [along_b(e), along_b(e, 1 - core)]
        else:
            second_in[core, 0] = block
            source, targets = second_in.at[core, 0], [None, twin]
        for n, device in enumerate(targets):
            if device is not None:
                c = copy(
                    source, second_in.at[core, e],
                    second_s.at[n, e], second_r.at[core, e], device,
                )
                c.start()
                second.append(c)
    for which in range(2):
        for e in order:
            if e:
                copy(
                    second_out.at[e], second_in.at[which, e],
                    second_s.at[0, e], second_r.at[which, e], twin,
                ).wait_recv()
    copy(
        second_out.at[1], second_in.at[1 - core, 0], second_s.at[1, 0],
        second_r.at[1 - core, 0], twin,
    ).wait_recv()
    halves = []
    for which in range(2):
        block = second_in[which, 0]
        for e in range(1, SIDE):
            block = block + second_in[which, e]
        halves.append(block)

    blocks = width // HEAD
    spacing = DEPTH // blocks
    offset = core * (spacing // 2)
    homes = [offset + (j % 2 * 2 + j // 2) * spacing for j in range(blocks)]

    def part_sent(j):
        @pl.when(z != homes[j])
        def _():
            copy(
                part.at[j], part_in.at[1], part_s.at[j], part_r.at[1], along_z(1)
            ).wait_send()

    loads[1].wait()
    for h in range(blocks // 2):
        columns = jnp.concatenate(
            [weight[:, (2 * n + h) * HEAD : (2 * n + h + 1) * HEAD] for n in range(2)], axis=1
        )
        product = jnp.dot(halves[0], columns[:half], preferred_element_type=F32) + jnp.dot(
            halves[1], columns[half:], preferred_element_type=F32
        )
        part[2 * h] = product[:, :HEAD]
        part[2 * h + 1] = product[:, HEAD:]
        if h:
            part_sent(2 * h - 2)
            part_sent(2 * h - 1)
        for j in (2 * h, 2 * h + 1):
            home = homes[j]
            d = lax.rem(home - z + DEPTH, DEPTH)

            @pl.when(d != 0)
            def _():
                copy(
                    part.at[j], part_in.at[d], part_s.at[j], part_r.at[d], at(x, y, core, home)
                ).start()

    is_home = lax.rem(z, spacing) == offset
    place = lax.div(z, spacing)
    my_block = lax.rem(place, 2) * 2 + lax.div(place, 2)

    @pl.when(is_home)
    def _():
        total = part[my_block]
        for d in range(1, DEPTH):
            copy(
                part.at[0], part_in.at[d], part_s.at[0], part_r.at[d], along_z(1)
            ).wait_recv()
            total = total + part_in[d]
        scale = lax.rsqrt(jnp.mean(total * total, axis=1, keepdims=True) + EPSILON)
        normed = total * scale * gain_ref[...]
        done[...] = jnp.where(my_block < blocks // 2, normed, total).astype(BF16)
        for d in range(1, DEPTH):
            copy(
                done, kv.at[core, my_block, b, a], column_s.at[d - 1],
                column_r.at[my_block], along_z(d),
            ).start()
        kv[core, my_block, b, a] = done[...]

    def row_copy(h, d):
        place = kv.at[core, pl.ds(2 * h, 2), b, a]
        return copy(place, place, row_s.at[h, d - 1], row_r.at[h, d - 1], along_a(d))

    def plane_copy(h, d):
        place = kv.at[core, pl.ds(2 * h, 2), b]
        return copy(place, place, plane_s.at[h, d - 1], plane_r.at[h, d - 1], along_b(d))

    def twin_copy(h, d):
        place = kv.at[core, pl.ds(2 * h, 2), lax.rem(b - d + SIDE, SIDE)]
        return copy(place, place, twin_s.at[h, d], twin_r.at[h, d], twin)

    others = range(1, SIDE)
    for h in range(blocks // 2):
        for j in (2 * h, 2 * h + 1):

            @pl.when(jnp.logical_not(is_home & (my_block == j)))
            def _():
                copy(
                    done, kv.at[core, j, b, a], column_s.at[0], column_r.at[j], along_z(1)
                ).wait_recv()

        for d in others:
            row_copy(h, d).start()
    for h in range(blocks // 2):
        for d in others:
            row_copy(h, d).wait_recv()
        for d in others:
            plane_copy(h, d).start()
        twin_copy(h, 0).start()

    loads[2].wait()
    rows = q_ref.shape[0]
    factor = HEAD**-0.5 * math.log2(math.e)

    def forward(h):
        for d in others:
            plane_copy(h, d).wait_recv()
            twin_copy(h, d).start()

    def arrived(h):
        for d in range(SIDE):
            twin_copy(h, d).wait_recv()

    key_heads = blocks // 2
    span = STEP_HEADS * rows

    def weigh(n, carry):
        which = lax.rem(core + lax.div(n, key_heads), 2)
        h = lax.rem(n, key_heads)

        @pl.when(n == 0)
        def _():
            forward(0)

        @pl.when(n == key_heads)
        def _():
            arrived(0)

        @pl.when(n == 2 * key_heads - 1)
        def _():
            forward(1)

        keys[:, :HEAD] = kv[which, h].reshape(PACKED, HEAD)
        keys[:, HEAD:] = hot[which]
        for i in range(GROUP // STEP_HEADS):
            head = (which * key_heads + h) * GROUP + i * STEP_HEADS
            base = pl.multiple_of(head * HEAD, HEAD)
            stacked = jnp.concatenate(
                [
                    jnp.concatenate([q_ref[:, pl.ds(base + m * HEAD, HEAD)], bias], axis=1)
                    for m in range(STEP_HEADS)
                ],
                axis=0,
            )
            scores = lax.dot_general(
                stacked, keys[...], (((1,), (1,)), ((), ())), preferred_element_type=F32
            )
            largest = jnp.maximum(jnp.max(scores, axis=1, keepdims=True), FLOOR_SCORE)
            weights = jnp.exp2(scores * factor - largest * factor)
            summed = jnp.sum(weights, axis=1, keepdims=True)
            rounded[n, i * span : (i + 1) * span] = weights.astype(BF16)
            divisor[n, i * span : (i + 1) * span] = jnp.broadcast_to(
                jnp.maximum(summed, 1.0), (span, HEAD)
            )
        return carry

    def mix(n, carry):
        which = lax.rem(core + lax.div(n, key_heads), 2)
        h = lax.rem(n, key_heads)

        @pl.when(n == key_heads)
        def _():
            arrived(1)

        mixed = jnp.dot(
            rounded[n], kv[which, key_heads + h].reshape(PACKED, HEAD), preferred_element_type=F32
        )
        out = (mixed / divisor[n]).astype(BF16)
        for m in range(GROUP):
            base = pl.multiple_of(((which * key_heads + h) * GROUP + m) * HEAD, HEAD)
            o_ref[:, pl.ds(base, HEAD)] = out[m * rows : (m + 1) * rows]
        return carry

    lax.fori_loop(0, 2 * key_heads, weigh, 0)
    lax.fori_loop(0, 2 * key_heads, mix, 0)

    for h in range(blocks // 2):
        for d in others:
            row_copy(h, d).wait_send()
            if True:
                plane_copy(h, d).wait_send()
        for d in range(SIDE):
            twin_copy(h, d).wait_send()
    for j in (blocks - 2, blocks - 1):
        part_sent(j)

    @pl.when(is_home)
    def _():
        for d in range(1, DEPTH):
            copy(
                done, kv.at[core, my_block, b, a], column_s.at[d - 1],
                column_r.at[my_block], along_z(d),
            ).wait_send()

    for c in to_twin + list(first.values()) + second:
        c.wait_send()


def shards(queries, vis_feats, kv_weight, key_gain, cross_mask, image_tokens, image_owner):
    half = vis_feats.shape[1] // 2
    blocks = kv_weight.shape[1] // (2 * HEAD)
    dma = pltpu.SemaphoreType.DMA
    whole = pl.BlockSpec(memory_space=pltpu.VMEM)
    stays = pl.BlockSpec(memory_space=pltpu.HBM)
    scalars = pl.BlockSpec(memory_space=pltpu.SMEM)
    return pl.pallas_call(
        kernel,
        out_shape=pltpu.VMEM(queries.shape, BF16),
        in_specs=[scalars, scalars, whole, whole, stays, stays, stays],
        out_specs=whole,
        scratch_shapes=[
            pltpu.VMEM(vis_feats.shape, BF16),
            pltpu.VMEM((kv_weight.shape[0], kv_weight.shape[1] // 2), BF16),
            pltpu.VMEM(queries.shape, BF16),
            pltpu.VMEM((SIDE, SIDE, SHARE, half), BF16),
            pltpu.VMEM((SIDE, SIDE, SHARE, half), BF16),
            pltpu.VMEM((SIDE, SIDE, SHARE, half), BF16),
            pltpu.VMEM((SIDE - 1, SIDE, SHARE, half), BF16),
            pltpu.VMEM((SIDE, SHARE, half), BF16),
            pltpu.VMEM((2, SIDE, SHARE, half), BF16),
            pltpu.VMEM((blocks, SHARE, HEAD), F32),
            pltpu.VMEM((DEPTH, SHARE, HEAD), F32),
            pltpu.VMEM((SHARE, HEAD), BF16),
            pltpu.VMEM((2, blocks, SIDE, SIDE, SHARE, HEAD), BF16),
            pltpu.VMEM((2, PACKED, HEAD), BF16),
            pltpu.VMEM((PACKED, 2 * HEAD), BF16),
            pltpu.VMEM((blocks, GROUP * queries.shape[0], PACKED), BF16),
            pltpu.VMEM((blocks, GROUP * queries.shape[0], HEAD), F32),
            dma((3,)),
            dma((SIDE,)), dma((SIDE,)),
            dma((SIDE - 1, SIDE)), dma((SIDE - 1, SIDE)),
            dma((2, SIDE)), dma((2, SIDE)),
            dma((blocks,)), dma((DEPTH,)),
            dma((DEPTH - 1,)), dma((blocks,)),
            dma((blocks // 2, SIDE - 1)), dma((blocks // 2, SIDE - 1)),
            dma((blocks // 2, SIDE - 1)), dma((blocks // 2, SIDE - 1)),
            dma((blocks // 2, SIDE)), dma((blocks // 2, SIDE)),
        ],
        compiler_params=pltpu.CompilerParams(
            collective_id=0, has_side_effects=True, vmem_limit_bytes=56 * 1024 * 1024
        ),
        name="cross_attend",
    )(
        image_tokens, image_owner, key_gain.reshape(1, HEAD), cross_mask.T, vis_feats, kv_weight,
        queries,
    )


def solution(mesh):
    return jax.shard_map(
        shards,
        mesh=mesh,
        in_specs=(
            P(("ctx", "head"), None),
            P("ctx", "head"),
            P("head", None),
            P(),
            P("ctx", None),
            P(),
            P(),
        ),
        out_specs=P(("ctx", "head"), None),
        check_vma=False,
    )
```

```python
import math

import jax
import jax.numpy as jnp
from jax import lax
from jax.experimental import pallas as pl
from jax.experimental.pallas import tpu as pltpu
from jax.sharding import PartitionSpec as P

EPSILON = 1e-05
FLOOR_SCORE = -1e30
MASKED = -(2.0**120)
HEAD = 128
SIDE = 4
DEPTH = 16
SHARE = 80
PACKED = SHARE * SIDE * SIDE
GROUP = 8
STEP_HEADS = 4
MESH = pl.DeviceIdType.MESH
BF16, F32 = jnp.bfloat16, jnp.float32


def kernel(
    tokens_ref, owner_ref, gain_ref, mask_ref, feats_hbm, weight_hbm, q_hbm, o_ref,
    feats, weight, q_ref, own, sib, first_sum, first_in, second_out, second_in, part, part_in,
    done, kv, hot, keys, rounded, divisor,
    load_s, sib_s, sib_r, first_s, first_r, second_s, second_r,
    part_s, part_r, column_s, column_r, row_s, row_r, plane_s, plane_r, twin_s, twin_r,
):
    ctx, z = lax.axis_index("ctx"), lax.axis_index("head")
    core = lax.rem(ctx, 2)
    x = lax.rem(lax.div(ctx, 2), SIDE)
    y = lax.div(ctx, 2 * SIDE)
    a = x * (1 - core) + y * core
    b = y * (1 - core) + x * core

    def at(x_to, y_to, core_to, z_to):
        return {"ctx": (y_to * SIDE + x_to) * 2 + core_to, "head": z_to}

    def along_a(d, core_to=core):
        to = lax.rem(a + d, SIDE)
        return at(to * (1 - core) + x * core, y * (1 - core) + to * core, core_to, z)

    def along_b(d, core_to=core):
        to = lax.rem(b + d, SIDE)
        return at(x * (1 - core) + to * core, to * (1 - core) + y * core, core_to, z)

    def along_z(d):
        return at(x, y, core, lax.rem(z + d, DEPTH))

    twin = at(x, y, 1 - core, z)

    def chip_of(which, a_to, b_to):
        return (a_to * SIDE + b_to) * (1 - which) + (b_to * SIDE + a_to) * which

    def copy(src, dst, send, recv, device):
        return pltpu.make_async_remote_copy(
            src_ref=src, dst_ref=dst, send_sem=send, recv_sem=recv,
            device_id=device, device_id_type=MESH,
        )

    barrier = pltpu.get_barrier_semaphore()
    greeted = (
        [twin]
        + [along_a(d) for d in range(1, SIDE)]
        + [along_b(d) for d in range(1, SIDE)]
        + [along_a(d, 1 - core) for d in range(1, SIDE)]
        + [along_z(d) for d in range(1, DEPTH)]
    )
    width = weight.shape[1]
    loads = [
        pltpu.make_async_copy(feats_hbm, feats, load_s.at[0]),
        pltpu.make_async_copy(
            weight_hbm.at[:, pl.ds(pl.multiple_of(core * width, width), width)],
            weight, load_s.at[1],
        ),
        pltpu.make_async_copy(q_hbm, q_ref, load_s.at[2]),
    ]
    loads[0].start()
    for device in greeted:
        pl.semaphore_signal(barrier, inc=1, device_id=device, device_id_type=MESH)
    for c in loads[1:]:
        c.start()

    images = tokens_ref.shape[0]
    starts, ends, total = [], [], jnp.int32(0)
    my_start, my_count = jnp.int32(0), jnp.int32(0)
    for i in range(images):
        starts.append(total)
        mine = owner_ref[i] == ctx
        my_start = jnp.where(mine, total, my_start)
        my_count = jnp.where(mine, tokens_ref[i], my_count)
        total = total + tokens_ref[i]
        ends.append(total)

    slots = feats.shape[0]
    half = feats.shape[1] // 2
    row_id = lax.broadcasted_iota(jnp.int32, (SHARE, slots), 0)
    slot_id = lax.broadcasted_iota(jnp.int32, (SHARE, slots), 1)
    distance = jnp.where(slot_id < my_count, row_id - slot_id, jnp.int32(1 << 20))

    def packed_rows(which, b_to, part_of):
        select = jnp.concatenate(
            [
                jnp.where(
                    distance == my_start - chip_of(which, a_to, b_to) * SHARE, 1.0, 0.0
                ).astype(BF16)
                for a_to in range(SIDE)
            ],
            axis=0,
        )
        columns = feats[:, pl.ds(pl.multiple_of(part_of * half, half), half)]
        rows_of = jnp.dot(select, columns, preferred_element_type=F32).astype(BF16)
        return rows_of.reshape(SIDE, SHARE, half)

    order = [2, 1, 3, 0]
    to_twin = [copy(own.at[e], sib.at[e], sib_s.at[e], sib_r.at[e], twin) for e in range(SIDE)]
    loads[0].wait()
    for n, e in enumerate(order):
        own[e] = packed_rows(1 - core, lax.rem(a + e, SIDE), 1 - core)
        if n == 0:
            pl.semaphore_wait(barrier, len(greeted))
        to_twin[e].start()
    for e in order:
        first_sum[e] = packed_rows(core, lax.rem(b + e, SIDE), core)
    first = {}
    for e in order:
        to_twin[e].wait_recv()
        first_sum[e] = first_sum[e] + sib[e]
        for d in (2, 1, 3):
            first[d, e] = copy(
                first_sum.at[e, lax.rem(a + d, SIDE)], first_in.at[d - 1, e],
                first_s.at[d - 1, e], first_r.at[d - 1, e], along_a(d),
            )
            first[d, e].start()

    lane = lax.broadcasted_iota(jnp.int32, (SHARE, HEAD), 1)
    row = lax.broadcasted_iota(jnp.int32, (SHARE, HEAD), 0)
    begin_of, end_of = jnp.zeros_like(lane), jnp.zeros_like(lane)
    for i in range(images):
        begin_of = jnp.where(lane == i, starts[i], begin_of)
        end_of = jnp.where(lane == i, ends[i], end_of)
    for which, a_from in ((core, a), (1 - core, b)):
        for b_to in range(SIDE):
            for e in range(SIDE):
                place = row + chip_of(which, lax.rem(a_from + e, SIDE), b_to) * SHARE
                inside = (place >= begin_of) & (place < end_of)
                base = (b_to * SIDE + e) * SHARE
                hot[which, base : base + SHARE, :] = jnp.where(inside, 1.0, 0.0).astype(BF16)
    bias_of = jnp.where(
        mask_ref[:, pl.ds(pl.multiple_of(z * HEAD, HEAD), HEAD)] == 1, 0.0, MASKED
    ).astype(BF16)
    same = lax.broadcasted_iota(jnp.int32, (images, HEAD), 0) == lax.broadcasted_iota(
        jnp.int32, (images, HEAD), 1
    )
    bias = lax.dot_general(
        bias_of, jnp.where(same, 1.0, 0.0).astype(BF16), (((0,), (0,)), ((), ())),
        preferred_element_type=F32,
    ).astype(BF16)

    second, arrivals = [], []
    for e in order:
        for d in range(1, SIDE):
            first[d, e].wait_recv()
        block = first_sum[e, a]
        for d in range(1, SIDE):
            block = block + first_in[d - 1, e]
        if e:
            second_out[e] = block
            source, targets = second_out.at[e], [along_b(e), along_b(e, 1 - core)]
        else:
            second_in[core, 0] = block
            source, targets = second_in.at[core, 0], [None, twin]
        for n, device in enumerate(targets):
            if device is not None:
                c = copy(
                    source, second_in.at[core, e],
                    second_s.at[n, e], second_r.at[core, e], device,
                )
                c.start()
                second.append(c)
    for which in range(2):
        for e in order:
            if e:
                copy(
                    second_out.at[e], second_in.at[which, e],
                    second_s.at[0, e], second_r.at[which, e], twin,
                ).wait_recv()
    copy(
        second_out.at[1], second_in.at[1 - core, 0], second_s.at[1, 0],
        second_r.at[1 - core, 0], twin,
    ).wait_recv()
    halves = []
    for which in range(2):
        block = second_in[which, 0]
        for e in range(1, SIDE):
            block = block + second_in[which, e]
        halves.append(block)

    blocks = width // HEAD
    spacing = DEPTH // blocks
    offset = core * (spacing // 2)
    homes = [offset + (j % 2 * 2 + j // 2) * spacing for j in range(blocks)]

    def part_sent(j):
        @pl.when(z != homes[j])
        def _():
            copy(
                part.at[j], part_in.at[1], part_s.at[j], part_r.at[1], along_z(1)
            ).wait_send()

    loads[1].wait()
    for h in range(blocks // 2):
        columns = jnp.concatenate(
            [weight[:, (2 * n + h) * HEAD : (2 * n + h + 1) * HEAD] for n in range(2)], axis=1
        )
        product = jnp.dot(halves[0], columns[:half], preferred_element_type=F32) + jnp.dot(
            halves[1], columns[half:], preferred_element_type=F32
        )
        part[2 * h] = product[:, :HEAD]
        part[2 * h + 1] = product[:, HEAD:]
        if h:
            part_sent(2 * h - 2)
            part_sent(2 * h - 1)
        for j in (2 * h, 2 * h + 1):
            home = homes[j]
            d = lax.rem(home - z + DEPTH, DEPTH)

            @pl.when(d != 0)
            def _():
                copy(
                    part.at[j], part_in.at[d], part_s.at[j], part_r.at[d], at(x, y, core, home)
                ).start()

    is_home = lax.rem(z, spacing) == offset
    place = lax.div(z, spacing)
    my_block = lax.rem(place, 2) * 2 + lax.div(place, 2)

    @pl.when(is_home)
    def _():
        total = part[my_block]
        for d in range(1, DEPTH):
            copy(
                part.at[0], part_in.at[d], part_s.at[0], part_r.at[d], along_z(1)
            ).wait_recv()
            total = total + part_in[d]
        scale = lax.rsqrt(jnp.mean(total * total, axis=1, keepdims=True) + EPSILON)
        normed = total * scale * gain_ref[...]
        done[...] = jnp.where(my_block < blocks // 2, normed, total).astype(BF16)
        for d in sorted(range(1, DEPTH), key=lambda d: -min(d, DEPTH - d)):
            copy(
                done, kv.at[core, my_block, b, 0], column_s.at[d - 1],
                column_r.at[my_block], along_z(d),
            ).start()
        kv[core, my_block, b, 0] = done[...]

    def row_copy(h, d):
        pieces = pl.ds(2 * h, 2)
        return copy(
            kv.at[core, pieces, b, 0], kv.at[core, pieces, b, SIDE - d],
            row_s.at[h, d - 1], row_r.at[h, d - 1], along_a(d),
        )

    def plane_copy(h, d, later):
        place = kv.at[core, pl.ds(2 * h, 2), b, pl.ds(1, SIDE - 1) if later else pl.ds(0, 1)]
        return copy(
            place, place, plane_s.at[h, later, d - 1], plane_r.at[h, later, d - 1], along_b(d)
        )

    def twin_copy(h, d):
        place = kv.at[core, pl.ds(2 * h, 2), lax.rem(b - d + SIDE, SIDE)]
        return copy(place, place, twin_s.at[h, d], twin_r.at[h, d], twin)

    others = sorted(range(1, SIDE), key=lambda d: -min(d, SIDE - d))
    for h in range(blocks // 2):
        for j in (2 * h, 2 * h + 1):

            @pl.when(jnp.logical_not(is_home & (my_block == j)))
            def _():
                copy(
                    done, kv.at[core, j, b, 0], column_s.at[0], column_r.at[j], along_z(1)
                ).wait_recv()

        for d in others:
            row_copy(h, d).start()
        for d in others:
            plane_copy(h, d, 0).start()
    for h in range(blocks // 2):
        for d in others:
            row_copy(h, d).wait_recv()
        for d in others:
            plane_copy(h, d, 1).start()
        twin_copy(h, 0).start()

    loads[2].wait()
    rows = q_ref.shape[0]
    factor = HEAD**-0.5 * math.log2(math.e)

    def forward(h):
        for d in others:
            plane_copy(h, d, 0).wait_recv()
            plane_copy(h, d, 1).wait_recv()
            twin_copy(h, d).start()

    def arrived(h):
        for d in range(SIDE):
            twin_copy(h, d).wait_recv()

    key_heads = blocks // 2
    span = STEP_HEADS * rows

    def weigh(n, carry):
        which = lax.rem(core + lax.div(n, key_heads), 2)
        h = lax.rem(n, key_heads)

        @pl.when(n == 0)
        def _():
            forward(0)

        @pl.when(n == key_heads)
        def _():
            arrived(0)

        @pl.when(n == key_heads)
        def _():
            forward(1)

        keys[:, :HEAD] = kv[which, h].reshape(PACKED, HEAD)
        keys[:, HEAD:] = hot[which]
        for i in range(GROUP // STEP_HEADS):
            head = (which * key_heads + h) * GROUP + i * STEP_HEADS
            base = pl.multiple_of(head * HEAD, HEAD)
            stacked = jnp.concatenate(
                [
                    jnp.concatenate([q_ref[:, pl.ds(base + m * HEAD, HEAD)], bias], axis=1)
                    for m in range(STEP_HEADS)
                ],
                axis=0,
            )
            scores = lax.dot_general(
                stacked, keys[...], (((1,), (1,)), ((), ())), preferred_element_type=F32
            )
            largest = jnp.maximum(jnp.max(scores, axis=1, keepdims=True), FLOOR_SCORE)
            weights = jnp.exp2(scores * factor - largest * factor)
            summed = jnp.sum(weights, axis=1, keepdims=True)
            rounded[n, i * span : (i + 1) * span] = weights.astype(BF16)
            divisor[n, i * span : (i + 1) * span] = jnp.broadcast_to(
                jnp.maximum(summed, 1.0), (span, HEAD)
            )
        return carry

    def mix(n, carry):
        which = lax.rem(core + lax.div(n, key_heads), 2)
        h = lax.rem(n, key_heads)

        @pl.when(n == key_heads)
        def _():
            arrived(1)

        mixed = jnp.dot(
            rounded[n], kv[which, key_heads + h].reshape(PACKED, HEAD), preferred_element_type=F32
        )
        out = (mixed / divisor[n]).astype(BF16)
        for m in range(GROUP):
            base = pl.multiple_of(((which * key_heads + h) * GROUP + m) * HEAD, HEAD)
            o_ref[:, pl.ds(base, HEAD)] = out[m * rows : (m + 1) * rows]
        return carry

    lax.fori_loop(0, 2 * key_heads, weigh, 0)
    lax.fori_loop(0, 2 * key_heads, mix, 0)

    for h in range(blocks // 2):
        for d in others:
            row_copy(h, d).wait_send()
            for later in range(2):
                plane_copy(h, d, later).wait_send()
        for d in range(SIDE):
            twin_copy(h, d).wait_send()
    for j in (blocks - 2, blocks - 1):
        part_sent(j)

    @pl.when(is_home)
    def _():
        for d in range(1, DEPTH):
            copy(
                done, kv.at[core, my_block, b, 0], column_s.at[d - 1],
                column_r.at[my_block], along_z(d),
            ).wait_send()

    for c in to_twin + list(first.values()) + second:
        c.wait_send()


def shards(queries, vis_feats, kv_weight, key_gain, cross_mask, image_tokens, image_owner):
    half = vis_feats.shape[1] // 2
    blocks = kv_weight.shape[1] // (2 * HEAD)
    dma = pltpu.SemaphoreType.DMA
    whole = pl.BlockSpec(memory_space=pltpu.VMEM)
    stays = pl.BlockSpec(memory_space=pltpu.HBM)
    scalars = pl.BlockSpec(memory_space=pltpu.SMEM)
    return pl.pallas_call(
        kernel,
        out_shape=pltpu.VMEM(queries.shape, BF16),
        in_specs=[scalars, scalars, whole, whole, stays, stays, stays],
        out_specs=whole,
        scratch_shapes=[
            pltpu.VMEM(vis_feats.shape, BF16),
            pltpu.VMEM((kv_weight.shape[0], kv_weight.shape[1] // 2), BF16),
            pltpu.VMEM(queries.shape, BF16),
            pltpu.VMEM((SIDE, SIDE, SHARE, half), BF16),
            pltpu.VMEM((SIDE, SIDE, SHARE, half), BF16),
            pltpu.VMEM((SIDE, SIDE, SHARE, half), BF16),
            pltpu.VMEM((SIDE - 1, SIDE, SHARE, half), BF16),
            pltpu.VMEM((SIDE, SHARE, half), BF16),
            pltpu.VMEM((2, SIDE, SHARE, half), BF16),
            pltpu.VMEM((blocks, SHARE, HEAD), F32),
            pltpu.VMEM((DEPTH, SHARE, HEAD), F32),
            pltpu.VMEM((SHARE, HEAD), BF16),
            pltpu.VMEM((2, blocks, SIDE, SIDE, SHARE, HEAD), BF16),
            pltpu.VMEM((2, PACKED, HEAD), BF16),
            pltpu.VMEM((PACKED, 2 * HEAD), BF16),
            pltpu.VMEM((blocks, GROUP * queries.shape[0], PACKED), BF16),
            pltpu.VMEM((blocks, GROUP * queries.shape[0], HEAD), F32),
            dma((3,)),
            dma((SIDE,)), dma((SIDE,)),
            dma((SIDE - 1, SIDE)), dma((SIDE - 1, SIDE)),
            dma((2, SIDE)), dma((2, SIDE)),
            dma((blocks,)), dma((DEPTH,)),
            dma((DEPTH - 1,)), dma((blocks,)),
            dma((blocks // 2, SIDE - 1)), dma((blocks // 2, SIDE - 1)),
            dma((blocks // 2, 2, SIDE - 1)), dma((blocks // 2, 2, SIDE - 1)),
            dma((blocks // 2, SIDE)), dma((blocks // 2, SIDE)),
        ],
        compiler_params=pltpu.CompilerParams(
            collective_id=0, has_side_effects=True, vmem_limit_bytes=56 * 1024 * 1024
        ),
        name="cross_attend",
    )(
        image_tokens, image_owner, key_gain.reshape(1, HEAD), cross_mask.T, vis_feats, kv_weight,
        queries,
    )


def solution(mesh):
    return jax.shard_map(
        shards,
        mesh=mesh,
        in_specs=(
            P(("ctx", "head"), None),
            P("ctx", "head"),
            P("head", None),
            P(),
            P("ctx", None),
            P(),
            P(),
        ),
        out_specs=P(("ctx", "head"), None),
        check_vma=False,
    )
```

```python
import math

import jax
import jax.numpy as jnp
from jax import lax
from jax.experimental import pallas as pl
from jax.experimental.pallas import tpu as pltpu
from jax.sharding import PartitionSpec as P

EPSILON = 1e-05
FLOOR_SCORE = -1e30
MASKED = -(2.0**120)
HEAD = 128
SIDE = 4
DEPTH = 16
SHARE = 80
PACKED = SHARE * SIDE * SIDE
GROUP = 8
STEP_HEADS = 4
MESH = pl.DeviceIdType.MESH
BF16, F32 = jnp.bfloat16, jnp.float32


def kernel(
    tokens_ref, owner_ref, gain_ref, mask_ref, feats_hbm, weight_hbm, q_hbm, o_ref,
    feats, weight, q_ref, own, sib, first_sum, first_in, second_out, second_in, part, part_in,
    done, kv, hot, keys, rounded, divisor,
    load_s, sib_s, sib_r, first_s, first_r, second_s, second_r,
    part_s, part_r, column_s, column_r, row_s, row_r, plane_s, plane_r, twin_s, twin_r,
):
    ctx, z = lax.axis_index("ctx"), lax.axis_index("head")
    core = lax.rem(ctx, 2)
    x = lax.rem(lax.div(ctx, 2), SIDE)
    y = lax.div(ctx, 2 * SIDE)
    a = x * (1 - core) + y * core
    b = y * (1 - core) + x * core

    def at(x_to, y_to, core_to, z_to):
        return {"ctx": (y_to * SIDE + x_to) * 2 + core_to, "head": z_to}

    def along_a(d, core_to=core):
        to = lax.rem(a + d, SIDE)
        return at(to * (1 - core) + x * core, y * (1 - core) + to * core, core_to, z)

    def along_b(d, core_to=core):
        to = lax.rem(b + d, SIDE)
        return at(x * (1 - core) + to * core, to * (1 - core) + y * core, core_to, z)

    def along_z(d):
        return at(x, y, core, lax.rem(z + d, DEPTH))

    twin = at(x, y, 1 - core, z)

    def chip_of(which, a_to, b_to):
        return (a_to * SIDE + b_to) * (1 - which) + (b_to * SIDE + a_to) * which

    def copy(src, dst, send, recv, device):
        return pltpu.make_async_remote_copy(
            src_ref=src, dst_ref=dst, send_sem=send, recv_sem=recv,
            device_id=device, device_id_type=MESH,
        )

    barrier = pltpu.get_barrier_semaphore()
    greeted = (
        [twin]
        + [along_a(d) for d in range(1, SIDE)]
        + [along_b(d) for d in range(1, SIDE)]
        + [along_a(d, 1 - core) for d in range(1, SIDE)]
        + [along_z(d) for d in range(1, DEPTH)]
    )
    width = weight.shape[1]
    loads = [
        pltpu.make_async_copy(feats_hbm, feats, load_s.at[0]),
        pltpu.make_async_copy(
            weight_hbm.at[:, pl.ds(pl.multiple_of(core * width, width), width)],
            weight, load_s.at[1],
        ),
        pltpu.make_async_copy(q_hbm, q_ref, load_s.at[2]),
    ]
    loads[0].start()
    for device in greeted:
        pl.semaphore_signal(barrier, inc=1, device_id=device, device_id_type=MESH)
    for c in loads[1:]:
        c.start()

    images = tokens_ref.shape[0]
    starts, ends, total = [], [], jnp.int32(0)
    my_start, my_count = jnp.int32(0), jnp.int32(0)
    for i in range(images):
        starts.append(total)
        mine = owner_ref[i] == ctx
        my_start = jnp.where(mine, total, my_start)
        my_count = jnp.where(mine, tokens_ref[i], my_count)
        total = total + tokens_ref[i]
        ends.append(total)

    slots = feats.shape[0]
    half = feats.shape[1] // 2
    row_id = lax.broadcasted_iota(jnp.int32, (SHARE, slots), 0)
    slot_id = lax.broadcasted_iota(jnp.int32, (SHARE, slots), 1)
    distance = jnp.where(slot_id < my_count, row_id - slot_id, jnp.int32(1 << 20))

    def packed_rows(which, b_to, part_of):
        select = jnp.concatenate(
            [
                jnp.where(
                    distance == my_start - chip_of(which, a_to, b_to) * SHARE, 1.0, 0.0
                ).astype(BF16)
                for a_to in range(SIDE)
            ],
            axis=0,
        )
        columns = feats[:, pl.ds(pl.multiple_of(part_of * half, half), half)]
        rows_of = jnp.dot(select, columns, preferred_element_type=F32).astype(BF16)
        return rows_of.reshape(SIDE, SHARE, half)

    order = [2, 1, 3, 0]
    to_twin = [copy(own.at[e], sib.at[e], sib_s.at[e], sib_r.at[e], twin) for e in range(SIDE)]
    loads[0].wait()
    for n, e in enumerate(order):
        own[e] = packed_rows(1 - core, lax.rem(a + e, SIDE), 1 - core)
        if n == 0:
            pl.semaphore_wait(barrier, len(greeted))
        to_twin[e].start()
    first = {}
    for e in order:
        packed = packed_rows(core, lax.rem(b + e, SIDE), core)
        to_twin[e].wait_recv()
        first_sum[e] = packed + sib[e]
        for d in (2, 1, 3):
            first[d, e] = copy(
                first_sum.at[e, lax.rem(a + d, SIDE)], first_in.at[d - 1, e],
                first_s.at[d - 1, e], first_r.at[d - 1, e], along_a(d),
            )
            first[d, e].start()

    lane = lax.broadcasted_iota(jnp.int32, (SHARE, HEAD), 1)
    row = lax.broadcasted_iota(jnp.int32, (SHARE, HEAD), 0)
    begin_of, end_of = jnp.zeros_like(lane), jnp.zeros_like(lane)
    for i in range(images):
        begin_of = jnp.where(lane == i, starts[i], begin_of)
        end_of = jnp.where(lane == i, ends[i], end_of)
    for which, a_from in ((core, a), (1 - core, b)):
        for b_to in range(SIDE):
            for e in range(SIDE):
                place = row + chip_of(which, lax.rem(a_from + e, SIDE), b_to) * SHARE
                inside = (place >= begin_of) & (place < end_of)
                base = (b_to * SIDE + e) * SHARE
                hot[which, base : base + SHARE, :] = jnp.where(inside, 1.0, 0.0).astype(BF16)
    bias_of = jnp.where(
        mask_ref[:, pl.ds(pl.multiple_of(z * HEAD, HEAD), HEAD)] == 1, 0.0, MASKED
    ).astype(BF16)
    same = lax.broadcasted_iota(jnp.int32, (images, HEAD), 0) == lax.broadcasted_iota(
        jnp.int32, (images, HEAD), 1
    )
    bias = lax.dot_general(
        bias_of, jnp.where(same, 1.0, 0.0).astype(BF16), (((0,), (0,)), ((), ())),
        preferred_element_type=F32,
    ).astype(BF16)

    second, arrivals = [], []
    for e in order:
        for d in range(1, SIDE):
            first[d, e].wait_recv()
        block = first_sum[e, a]
        for d in range(1, SIDE):
            block = block + first_in[d - 1, e]
        if e:
            second_out[e] = block
            source, targets = second_out.at[e], [along_b(e), along_b(e, 1 - core)]
        else:
            second_in[core, 0] = block
            source, targets = second_in.at[core, 0], [None, twin]
        for n, device in enumerate(targets):
            if device is not None:
                c = copy(
                    source, second_in.at[core, e],
                    second_s.at[n, e], second_r.at[core, e], device,
                )
                c.start()
                second.append(c)
    for which in range(2):
        for e in order:
            if e:
                copy(
                    second_out.at[e], second_in.at[which, e],
                    second_s.at[0, e], second_r.at[which, e], twin,
                ).wait_recv()
    copy(
        second_out.at[1], second_in.at[1 - core, 0], second_s.at[1, 0],
        second_r.at[1 - core, 0], twin,
    ).wait_recv()
    halves = []
    for which in range(2):
        block = second_in[which, 0]
        for e in range(1, SIDE):
            block = block + second_in[which, e]
        halves.append(block)

    blocks = width // HEAD
    spacing = DEPTH // blocks
    offset = core * (spacing // 2)
    homes = [offset + (j % 2 * 2 + j // 2) * spacing for j in range(blocks)]

    def part_sent(j):
        @pl.when(z != homes[j])
        def _():
            copy(
                part.at[j], part_in.at[1], part_s.at[j], part_r.at[1], along_z(1)
            ).wait_send()

    loads[1].wait()
    for h in range(blocks // 2):
        columns = jnp.concatenate(
            [weight[:, (2 * n + h) * HEAD : (2 * n + h + 1) * HEAD] for n in range(2)], axis=1
        )
        product = jnp.dot(halves[0], columns[:half], preferred_element_type=F32) + jnp.dot(
            halves[1], columns[half:], preferred_element_type=F32
        )
        part[2 * h] = product[:, :HEAD]
        part[2 * h + 1] = product[:, HEAD:]
        if h:
            part_sent(2 * h - 2)
            part_sent(2 * h - 1)
        for j in (2 * h, 2 * h + 1):
            home = homes[j]
            d = lax.rem(home - z + DEPTH, DEPTH)

            @pl.when(d != 0)
            def _():
                copy(
                    part.at[j], part_in.at[d], part_s.at[j], part_r.at[d], at(x, y, core, home)
                ).start()

    is_home = lax.rem(z, spacing) == offset
    place = lax.div(z, spacing)
    my_block = lax.rem(place, 2) * 2 + lax.div(place, 2)

    @pl.when(is_home)
    def _():
        total = part[my_block]
        for d in range(1, DEPTH):
            copy(
                part.at[0], part_in.at[d], part_s.at[0], part_r.at[d], along_z(1)
            ).wait_recv()
            total = total + part_in[d]
        scale = lax.rsqrt(jnp.mean(total * total, axis=1, keepdims=True) + EPSILON)
        normed = total * scale * gain_ref[...]
        done[...] = jnp.where(my_block < blocks // 2, normed, total).astype(BF16)
        for d in sorted(range(1, DEPTH), key=lambda d: -min(d, DEPTH - d)):
            copy(
                done, kv.at[core, my_block, b, 0], column_s.at[d - 1],
                column_r.at[my_block], along_z(d),
            ).start()
        kv[core, my_block, b, 0] = done[...]

    def row_copy(h, d):
        pieces = pl.ds(2 * h, 2)
        return copy(
            kv.at[core, pieces, b, 0], kv.at[core, pieces, b, SIDE - d],
            row_s.at[h, d - 1], row_r.at[h, d - 1], along_a(d),
        )

    def plane_copy(h, d, later):
        place = kv.at[core, pl.ds(2 * h, 2), b, pl.ds(1, SIDE - 1) if later else pl.ds(0, 1)]
        return copy(
            place, place, plane_s.at[h, later, d - 1], plane_r.at[h, later, d - 1], along_b(d)
        )

    def twin_copy(h, d):
        place = kv.at[core, pl.ds(2 * h, 2), lax.rem(b - d + SIDE, SIDE)]
        return copy(place, place, twin_s.at[h, d], twin_r.at[h, d], twin)

    others = sorted(range(1, SIDE), key=lambda d: -min(d, SIDE - d))
    for h in range(blocks // 2):
        for j in (2 * h, 2 * h + 1):

            @pl.when(jnp.logical_not(is_home & (my_block == j)))
            def _():
                copy(
                    done, kv.at[core, j, b, 0], column_s.at[0], column_r.at[j], along_z(1)
                ).wait_recv()

        for d in others:
            row_copy(h, d).start()
        for d in others:
            plane_copy(h, d, 0).start()
    for h in range(blocks // 2):
        for d in others:
            row_copy(h, d).wait_recv()
        for d in others:
            plane_copy(h, d, 1).start()
        twin_copy(h, 0).start()

    loads[2].wait()
    rows = q_ref.shape[0]
    factor = HEAD**-0.5 * math.log2(math.e)

    def forward(h):
        for d in others:
            plane_copy(h, d, 0).wait_recv()
            plane_copy(h, d, 1).wait_recv()
            twin_copy(h, d).start()

    def arrived(h):
        for d in range(SIDE):
            twin_copy(h, d).wait_recv()

    key_heads = blocks // 2
    span = STEP_HEADS * rows

    def weigh(n, carry):
        which = lax.rem(core + lax.div(n, key_heads), 2)
        h = lax.rem(n, key_heads)

        @pl.when(n == 0)
        def _():
            forward(0)

        @pl.when(n == key_heads)
        def _():
            arrived(0)

        @pl.when(n == key_heads)
        def _():
            forward(1)

        keys[:, :HEAD] = kv[which, h].reshape(PACKED, HEAD)
        keys[:, HEAD:] = hot[which]
        for i in range(GROUP // STEP_HEADS):
            head = (which * key_heads + h) * GROUP + i * STEP_HEADS
            base = pl.multiple_of(head * HEAD, HEAD)
            stacked = jnp.concatenate(
                [
                    jnp.concatenate([q_ref[:, pl.ds(base + m * HEAD, HEAD)], bias], axis=1)
                    for m in range(STEP_HEADS)
                ],
                axis=0,
            )
            scores = lax.dot_general(
                stacked, keys[...], (((1,), (1,)), ((), ())), preferred_element_type=F32
            )
            largest = jnp.maximum(jnp.max(scores, axis=1, keepdims=True), FLOOR_SCORE)
            weights = jnp.exp2(scores * factor - largest * factor)
            summed = jnp.sum(weights, axis=1, keepdims=True)
            rounded[n, i * span : (i + 1) * span] = weights.astype(BF16)
            divisor[n, i * span : (i + 1) * span] = jnp.broadcast_to(
                jnp.maximum(summed, 1.0), (span, HEAD)
            )
        return carry

    def mix(n, carry):
        which = lax.rem(core + lax.div(n, key_heads), 2)
        h = lax.rem(n, key_heads)

        @pl.when(n == key_heads)
        def _():
            arrived(1)

        mixed = jnp.dot(
            rounded[n], kv[which, key_heads + h].reshape(PACKED, HEAD), preferred_element_type=F32
        )
        out = (mixed / divisor[n]).astype(BF16)
        for m in range(GROUP):
            base = pl.multiple_of(((which * key_heads + h) * GROUP + m) * HEAD, HEAD)
            o_ref[:, pl.ds(base, HEAD)] = out[m * rows : (m + 1) * rows]
        return carry

    lax.fori_loop(0, 2 * key_heads, weigh, 0)
    lax.fori_loop(0, 2 * key_heads, mix, 0)

    for h in range(blocks // 2):
        for d in others:
            row_copy(h, d).wait_send()
            for later in range(2):
                plane_copy(h, d, later).wait_send()
        for d in range(SIDE):
            twin_copy(h, d).wait_send()
    for j in (blocks - 2, blocks - 1):
        part_sent(j)

    @pl.when(is_home)
    def _():
        for d in range(1, DEPTH):
            copy(
                done, kv.at[core, my_block, b, 0], column_s.at[d - 1],
                column_r.at[my_block], along_z(d),
            ).wait_send()

    for c in to_twin + list(first.values()) + second:
        c.wait_send()


def shards(queries, vis_feats, kv_weight, key_gain, cross_mask, image_tokens, image_owner):
    half = vis_feats.shape[1] // 2
    blocks = kv_weight.shape[1] // (2 * HEAD)
    dma = pltpu.SemaphoreType.DMA
    whole = pl.BlockSpec(memory_space=pltpu.VMEM)
    stays = pl.BlockSpec(memory_space=pltpu.HBM)
    scalars = pl.BlockSpec(memory_space=pltpu.SMEM)
    return pl.pallas_call(
        kernel,
        out_shape=pltpu.VMEM(queries.shape, BF16),
        in_specs=[scalars, scalars, whole, whole, stays, stays, stays],
        out_specs=whole,
        scratch_shapes=[
            pltpu.VMEM(vis_feats.shape, BF16),
            pltpu.VMEM((kv_weight.shape[0], kv_weight.shape[1] // 2), BF16),
            pltpu.VMEM(queries.shape, BF16),
            pltpu.VMEM((SIDE, SIDE, SHARE, half), BF16),
            pltpu.VMEM((SIDE, SIDE, SHARE, half), BF16),
            pltpu.VMEM((SIDE, SIDE, SHARE, half), BF16),
            pltpu.VMEM((SIDE - 1, SIDE, SHARE, half), BF16),
            pltpu.VMEM((SIDE, SHARE, half), BF16),
            pltpu.VMEM((2, SIDE, SHARE, half), BF16),
            pltpu.VMEM((blocks, SHARE, HEAD), F32),
            pltpu.VMEM((DEPTH, SHARE, HEAD), F32),
            pltpu.VMEM((SHARE, HEAD), BF16),
            pltpu.VMEM((2, blocks, SIDE, SIDE, SHARE, HEAD), BF16),
            pltpu.VMEM((2, PACKED, HEAD), BF16),
            pltpu.VMEM((PACKED, 2 * HEAD), BF16),
            pltpu.VMEM((blocks, GROUP * queries.shape[0], PACKED), BF16),
            pltpu.VMEM((blocks, GROUP * queries.shape[0], HEAD), F32),
            dma((3,)),
            dma((SIDE,)), dma((SIDE,)),
            dma((SIDE - 1, SIDE)), dma((SIDE - 1, SIDE)),
            dma((2, SIDE)), dma((2, SIDE)),
            dma((blocks,)), dma((DEPTH,)),
            dma((DEPTH - 1,)), dma((blocks,)),
            dma((blocks // 2, SIDE - 1)), dma((blocks // 2, SIDE - 1)),
            dma((blocks // 2, 2, SIDE - 1)), dma((blocks // 2, 2, SIDE - 1)),
            dma((blocks // 2, SIDE)), dma((blocks // 2, SIDE)),
        ],
        compiler_params=pltpu.CompilerParams(
            collective_id=0, has_side_effects=True, vmem_limit_bytes=56 * 1024 * 1024
        ),
        name="cross_attend",
    )(
        image_tokens, image_owner, key_gain.reshape(1, HEAD), cross_mask.T, vis_feats, kv_weight,
        queries,
    )


def solution(mesh):
    return jax.shard_map(
        shards,
        mesh=mesh,
        in_specs=(
            P(("ctx", "head"), None),
            P("ctx", "head"),
            P("head", None),
            P(),
            P("ctx", None),
            P(),
            P(),
        ),
        out_specs=P(("ctx", "head"), None),
        check_vma=False,
    )
```

```python
import math

import jax
import jax.numpy as jnp
from jax import lax
from jax.experimental import pallas as pl
from jax.experimental.pallas import tpu as pltpu
from jax.sharding import PartitionSpec as P

EPSILON = 1e-05
FLOOR_SCORE = -1e30
MASKED = -(2.0**120)
HEAD = 128
SIDE = 4
DEPTH = 16
SHARE = 80
PACKED = SHARE * SIDE * SIDE
GROUP = 8
STEP_HEADS = 4
MESH = pl.DeviceIdType.MESH
BF16, F32 = jnp.bfloat16, jnp.float32


def kernel(
    tokens_ref, owner_ref, gain_ref, mask_ref, feats_hbm, weight_hbm, q_hbm, o_ref,
    feats, weight, q_ref, own, sib, first_sum, first_in, second_out, second_in, part, part_in,
    done, kv, hot, keys, rounded, divisor,
    load_s, sib_s, sib_r, first_s, first_r, second_s, second_r,
    part_s, part_r, column_s, column_r, row_s, row_r, plane_s, plane_r, twin_s, twin_r,
):
    ctx, z = lax.axis_index("ctx"), lax.axis_index("head")
    core = lax.rem(ctx, 2)
    x = lax.rem(lax.div(ctx, 2), SIDE)
    y = lax.div(ctx, 2 * SIDE)
    a = x * (1 - core) + y * core
    b = y * (1 - core) + x * core

    def at(x_to, y_to, core_to, z_to):
        return {"ctx": (y_to * SIDE + x_to) * 2 + core_to, "head": z_to}

    def along_a(d, core_to=core):
        to = lax.rem(a + d, SIDE)
        return at(to * (1 - core) + x * core, y * (1 - core) + to * core, core_to, z)

    def along_b(d, core_to=core):
        to = lax.rem(b + d, SIDE)
        return at(x * (1 - core) + to * core, to * (1 - core) + y * core, core_to, z)

    def along_z(d):
        return at(x, y, core, lax.rem(z + d, DEPTH))

    twin = at(x, y, 1 - core, z)

    def chip_of(which, a_to, b_to):
        return (a_to * SIDE + b_to) * (1 - which) + (b_to * SIDE + a_to) * which

    def copy(src, dst, send, recv, device):
        return pltpu.make_async_remote_copy(
            src_ref=src, dst_ref=dst, send_sem=send, recv_sem=recv,
            device_id=device, device_id_type=MESH,
        )

    barrier = pltpu.get_barrier_semaphore()
    far_first = sorted(range(1, DEPTH), key=lambda d: -min(d, DEPTH - d))
    greeted = [along_z(d) for d in far_first]
    for d in (2, 1, 3):
        greeted += [along_a(d), along_b(d), along_a(d, 1 - core)]
    greeted.append(twin)
    width = weight.shape[1]
    loads = [
        pltpu.make_async_copy(feats_hbm, feats, load_s.at[0]),
        pltpu.make_async_copy(
            weight_hbm.at[:, pl.ds(pl.multiple_of(core * width, width), width)],
            weight, load_s.at[1],
        ),
        pltpu.make_async_copy(q_hbm, q_ref, load_s.at[2]),
    ]
    loads[0].start()
    for device in greeted:
        pl.semaphore_signal(barrier, inc=1, device_id=device, device_id_type=MESH)
    for c in loads[1:]:
        c.start()

    images = tokens_ref.shape[0]
    starts, ends, total = [], [], jnp.int32(0)
    my_start, my_count = jnp.int32(0), jnp.int32(0)
    for i in range(images):
        starts.append(total)
        mine = owner_ref[i] == ctx
        my_start = jnp.where(mine, total, my_start)
        my_count = jnp.where(mine, tokens_ref[i], my_count)
        total = total + tokens_ref[i]
        ends.append(total)

    slots = feats.shape[0]
    half = feats.shape[1] // 2
    row_id = lax.broadcasted_iota(jnp.int32, (SHARE, slots), 0)
    slot_id = lax.broadcasted_iota(jnp.int32, (SHARE, slots), 1)
    distance = jnp.where(slot_id < my_count, row_id - slot_id, jnp.int32(1 << 20))

    def packed_rows(which, b_to, part_of):
        select = jnp.concatenate(
            [
                jnp.where(
                    distance == my_start - chip_of(which, a_to, b_to) * SHARE, 1.0, 0.0
                ).astype(BF16)
                for a_to in range(SIDE)
            ],
            axis=0,
        )
        columns = feats[:, pl.ds(pl.multiple_of(part_of * half, half), half)]
        rows_of = jnp.dot(select, columns, preferred_element_type=F32).astype(BF16)
        return rows_of.reshape(SIDE, SHARE, half)

    order = [2, 1, 3, 0]
    to_twin = [copy(own.at[e], sib.at[e], sib_s.at[e], sib_r.at[e], twin) for e in range(SIDE)]
    loads[0].wait()
    for n, e in enumerate(order):
        own[e] = packed_rows(1 - core, lax.rem(a + e, SIDE), 1 - core)
        if n == 0:
            pl.semaphore_wait(barrier, len(greeted))
        to_twin[e].start()
    first = {}
    for e in order:
        packed = packed_rows(core, lax.rem(b + e, SIDE), core)
        to_twin[e].wait_recv()
        first_sum[e] = packed + sib[e]
        for d in (2, 1, 3):
            first[d, e] = copy(
                first_sum.at[e, lax.rem(a + d, SIDE)], first_in.at[d - 1, e],
                first_s.at[d - 1, e], first_r.at[d - 1, e], along_a(d),
            )
            first[d, e].start()

    lane = lax.broadcasted_iota(jnp.int32, (SHARE, HEAD), 1)
    row = lax.broadcasted_iota(jnp.int32, (SHARE, HEAD), 0)
    begin_of, end_of = jnp.zeros_like(lane), jnp.zeros_like(lane)
    for i in range(images):
        begin_of = jnp.where(lane == i, starts[i], begin_of)
        end_of = jnp.where(lane == i, ends[i], end_of)
    for which, a_from in ((core, a), (1 - core, b)):
        for b_to in range(SIDE):
            for e in range(SIDE):
                place = row + chip_of(which, lax.rem(a_from + e, SIDE), b_to) * SHARE
                inside = (place >= begin_of) & (place < end_of)
                base = (b_to * SIDE + e) * SHARE
                hot[which, base : base + SHARE, :] = jnp.where(inside, 1.0, 0.0).astype(BF16)
    bias_of = jnp.where(
        mask_ref[:, pl.ds(pl.multiple_of(z * HEAD, HEAD), HEAD)] == 1, 0.0, MASKED
    ).astype(BF16)
    same = lax.broadcasted_iota(jnp.int32, (images, HEAD), 0) == lax.broadcasted_iota(
        jnp.int32, (images, HEAD), 1
    )
    bias = lax.dot_general(
        bias_of, jnp.where(same, 1.0, 0.0).astype(BF16), (((0,), (0,)), ((), ())),
        preferred_element_type=F32,
    ).astype(BF16)

    second, arrivals = [], []
    for e in order:
        for d in range(1, SIDE):
            first[d, e].wait_recv()
        block = first_sum[e, a]
        for d in range(1, SIDE):
            block = block + first_in[d - 1, e]
        if e:
            second_out[e] = block
            source, targets = second_out.at[e], [along_b(e), along_b(e, 1 - core)]
        else:
            second_in[core, 0] = block
            source, targets = second_in.at[core, 0], [None, twin]
        for n, device in enumerate(targets):
            if device is not None:
                c = copy(
                    source, second_in.at[core, e],
                    second_s.at[n, e], second_r.at[core, e], device,
                )
                c.start()
                second.append(c)
    for which in range(2):
        for e in order:
            if e:
                copy(
                    second_out.at[e], second_in.at[which, e],
                    second_s.at[0, e], second_r.at[which, e], twin,
                ).wait_recv()
    copy(
        second_out.at[1], second_in.at[1 - core, 0], second_s.at[1, 0],
        second_r.at[1 - core, 0], twin,
    ).wait_recv()
    halves = []
    for which in range(2):
        block = second_in[which, 0]
        for e in range(1, SIDE):
            block = block + second_in[which, e]
        halves.append(block)

    blocks = width // HEAD
    spacing = DEPTH // blocks
    offset = core * (spacing // 2)
    homes = [offset + (j % 2 * 2 + j // 2) * spacing for j in range(blocks)]

    def part_sent(j):
        @pl.when(z != homes[j])
        def _():
            copy(
                part.at[j], part_in.at[1], part_s.at[j], part_r.at[1], along_z(1)
            ).wait_send()

    loads[1].wait()
    for h in range(blocks // 2):
        columns = jnp.concatenate(
            [weight[:, (2 * n + h) * HEAD : (2 * n + h + 1) * HEAD] for n in range(2)], axis=1
        )
        product = jnp.dot(halves[0], columns[:half], preferred_element_type=F32) + jnp.dot(
            halves[1], columns[half:], preferred_element_type=F32
        )
        part[2 * h] = product[:, :HEAD]
        part[2 * h + 1] = product[:, HEAD:]
        if h:
            part_sent(2 * h - 2)
            part_sent(2 * h - 1)
        for j in (2 * h, 2 * h + 1):
            home = homes[j]
            d = lax.rem(home - z + DEPTH, DEPTH)

            @pl.when(d != 0)
            def _():
                copy(
                    part.at[j], part_in.at[d], part_s.at[j], part_r.at[d], at(x, y, core, home)
                ).start()

    is_home = lax.rem(z, spacing) == offset
    place = lax.div(z, spacing)
    my_block = lax.rem(place, 2) * 2 + lax.div(place, 2)

    @pl.when(is_home)
    def _():
        total = part[my_block]
        for d in range(1, DEPTH):
            copy(
                part.at[0], part_in.at[d], part_s.at[0], part_r.at[d], along_z(1)
            ).wait_recv()
            total = total + part_in[d]
        scale = lax.rsqrt(jnp.mean(total * total, axis=1, keepdims=True) + EPSILON)
        normed = total * scale * gain_ref[...]
        done[...] = jnp.where(my_block < blocks // 2, normed, total).astype(BF16)
        for d in sorted(range(1, DEPTH), key=lambda d: -min(d, DEPTH - d)):
            copy(
                done, kv.at[core, my_block, b, 0], column_s.at[d - 1],
                column_r.at[my_block], along_z(d),
            ).start()
        kv[core, my_block, b, 0] = done[...]

    def row_copy(h, d):
        pieces = pl.ds(2 * h, 2)
        return copy(
            kv.at[core, pieces, b, 0], kv.at[core, pieces, b, SIDE - d],
            row_s.at[h, d - 1], row_r.at[h, d - 1], along_a(d),
        )

    def plane_copy(h, d, later):
        place = kv.at[core, pl.ds(2 * h, 2), b, pl.ds(1, SIDE - 1) if later else pl.ds(0, 1)]
        return copy(
            place, place, plane_s.at[h, later, d - 1], plane_r.at[h, later, d - 1], along_b(d)
        )

    def twin_copy(h, d):
        place = kv.at[core, pl.ds(2 * h, 2), lax.rem(b - d + SIDE, SIDE)]
        return copy(place, place, twin_s.at[h, d], twin_r.at[h, d], twin)

    others = sorted(range(1, SIDE), key=lambda d: -min(d, SIDE - d))
    for h in range(blocks // 2):
        for j in (2 * h, 2 * h + 1):

            @pl.when(jnp.logical_not(is_home & (my_block == j)))
            def _():
                copy(
                    done, kv.at[core, j, b, 0], column_s.at[0], column_r.at[j], along_z(1)
                ).wait_recv()

        for d in others:
            row_copy(h, d).start()
        for d in others:
            plane_copy(h, d, 0).start()
    for h in range(blocks // 2):
        for d in others:
            row_copy(h, d).wait_recv()
        for d in others:
            plane_copy(h, d, 1).start()
        twin_copy(h, 0).start()

    loads[2].wait()
    rows = q_ref.shape[0]
    factor = HEAD**-0.5 * math.log2(math.e)

    def forward(h):
        for d in others:
            plane_copy(h, d, 0).wait_recv()
            plane_copy(h, d, 1).wait_recv()
            twin_copy(h, d).start()

    def arrived(h):
        for d in range(SIDE):
            twin_copy(h, d).wait_recv()

    key_heads = blocks // 2
    span = STEP_HEADS * rows

    def weigh(n, carry):
        which = lax.rem(core + lax.div(n, key_heads), 2)
        h = lax.rem(n, key_heads)

        @pl.when(n == 0)
        def _():
            forward(0)

        @pl.when(n == key_heads)
        def _():
            arrived(0)

        @pl.when(n == key_heads)
        def _():
            forward(1)

        keys[:, :HEAD] = kv[which, h].reshape(PACKED, HEAD)
        keys[:, HEAD:] = hot[which]
        for i in range(GROUP // STEP_HEADS):
            head = (which * key_heads + h) * GROUP + i * STEP_HEADS
            base = pl.multiple_of(head * HEAD, HEAD)
            stacked = jnp.concatenate(
                [
                    jnp.concatenate([q_ref[:, pl.ds(base + m * HEAD, HEAD)], bias], axis=1)
                    for m in range(STEP_HEADS)
                ],
                axis=0,
            )
            scores = lax.dot_general(
                stacked, keys[...], (((1,), (1,)), ((), ())), preferred_element_type=F32
            )
            largest = jnp.maximum(jnp.max(scores, axis=1, keepdims=True), FLOOR_SCORE)
            weights = jnp.exp2(scores * factor - largest * factor)
            summed = jnp.sum(weights, axis=1, keepdims=True)
            rounded[n, i * span : (i + 1) * span] = weights.astype(BF16)
            divisor[n, i * span : (i + 1) * span] = jnp.broadcast_to(
                jnp.maximum(summed, 1.0), (span, HEAD)
            )
        return carry

    def mix(n, carry):
        which = lax.rem(core + lax.div(n, key_heads), 2)
        h = lax.rem(n, key_heads)

        @pl.when(n == key_heads)
        def _():
            arrived(1)

        mixed = jnp.dot(
            rounded[n], kv[which, key_heads + h].reshape(PACKED, HEAD), preferred_element_type=F32
        )
        out = (mixed / divisor[n]).astype(BF16)
        for m in range(GROUP):
            base = pl.multiple_of(((which * key_heads + h) * GROUP + m) * HEAD, HEAD)
            o_ref[:, pl.ds(base, HEAD)] = out[m * rows : (m + 1) * rows]
        return carry

    lax.fori_loop(0, 2 * key_heads, weigh, 0)
    lax.fori_loop(0, 2 * key_heads, mix, 0)

    for h in range(blocks // 2):
        for d in others:
            row_copy(h, d).wait_send()
            for later in range(2):
                plane_copy(h, d, later).wait_send()
        for d in range(SIDE):
            twin_copy(h, d).wait_send()
    for j in (blocks - 2, blocks - 1):
        part_sent(j)

    @pl.when(is_home)
    def _():
        for d in range(1, DEPTH):
            copy(
                done, kv.at[core, my_block, b, 0], column_s.at[d - 1],
                column_r.at[my_block], along_z(d),
            ).wait_send()

    for c in to_twin + list(first.values()) + second:
        c.wait_send()


def shards(queries, vis_feats, kv_weight, key_gain, cross_mask, image_tokens, image_owner):
    half = vis_feats.shape[1] // 2
    blocks = kv_weight.shape[1] // (2 * HEAD)
    dma = pltpu.SemaphoreType.DMA
    whole = pl.BlockSpec(memory_space=pltpu.VMEM)
    stays = pl.BlockSpec(memory_space=pltpu.HBM)
    scalars = pl.BlockSpec(memory_space=pltpu.SMEM)
    return pl.pallas_call(
        kernel,
        out_shape=pltpu.VMEM(queries.shape, BF16),
        in_specs=[scalars, scalars, whole, whole, stays, stays, stays],
        out_specs=whole,
        scratch_shapes=[
            pltpu.VMEM(vis_feats.shape, BF16),
            pltpu.VMEM((kv_weight.shape[0], kv_weight.shape[1] // 2), BF16),
            pltpu.VMEM(queries.shape, BF16),
            pltpu.VMEM((SIDE, SIDE, SHARE, half), BF16),
            pltpu.VMEM((SIDE, SIDE, SHARE, half), BF16),
            pltpu.VMEM((SIDE, SIDE, SHARE, half), BF16),
            pltpu.VMEM((SIDE - 1, SIDE, SHARE, half), BF16),
            pltpu.VMEM((SIDE, SHARE, half), BF16),
            pltpu.VMEM((2, SIDE, SHARE, half), BF16),
            pltpu.VMEM((blocks, SHARE, HEAD), F32),
            pltpu.VMEM((DEPTH, SHARE, HEAD), F32),
            pltpu.VMEM((SHARE, HEAD), BF16),
            pltpu.VMEM((2, blocks, SIDE, SIDE, SHARE, HEAD), BF16),
            pltpu.VMEM((2, PACKED, HEAD), BF16),
            pltpu.VMEM((PACKED, 2 * HEAD), BF16),
            pltpu.VMEM((blocks, GROUP * queries.shape[0], PACKED), BF16),
            pltpu.VMEM((blocks, GROUP * queries.shape[0], HEAD), F32),
            dma((3,)),
            dma((SIDE,)), dma((SIDE,)),
            dma((SIDE - 1, SIDE)), dma((SIDE - 1, SIDE)),
            dma((2, SIDE)), dma((2, SIDE)),
            dma((blocks,)), dma((DEPTH,)),
            dma((DEPTH - 1,)), dma((blocks,)),
            dma((blocks // 2, SIDE - 1)), dma((blocks // 2, SIDE - 1)),
            dma((blocks // 2, 2, SIDE - 1)), dma((blocks // 2, 2, SIDE - 1)),
            dma((blocks // 2, SIDE)), dma((blocks // 2, SIDE)),
        ],
        compiler_params=pltpu.CompilerParams(
            collective_id=0, has_side_effects=True, vmem_limit_bytes=56 * 1024 * 1024
        ),
        name="cross_attend",
    )(
        image_tokens, image_owner, key_gain.reshape(1, HEAD), cross_mask.T, vis_feats, kv_weight,
        queries,
    )


def solution(mesh):
    return jax.shard_map(
        shards,
        mesh=mesh,
        in_specs=(
            P(("ctx", "head"), None),
            P("ctx", "head"),
            P("head", None),
            P(),
            P("ctx", None),
            P(),
            P(),
        ),
        out_specs=P(("ctx", "head"), None),
        check_vma=False,
    )
```
